128 devices in a mesh: seq: 16 (over x, z), head: 8 (over y, core).
Axes of the slice: x: 4, y: 4, z: 4, core: 2. Of those that a mesh axis runs over, the one named last changes fastest.
Arguments:
- queries: float32 [4096, 8192], P('seq', 'head'), may hold values from -8 to 8
- key_heads: float32 [4096, 1024], P('seq', 'head'), may hold values from -6 to 6
- value_heads: float32 [4096, 1024], P('seq', 'head'), may hold values from -6 to 6
- query_map: float32 [64, 128, 128], P('head'), may hold values from -0.5 to 0.5
- key_map: float32 [8, 128, 128], P('head'), may hold values from -0.5 to 0.5
Outputs:
- query_map_step: float32 [64, 128, 128], P('head')
- key_map_step: float32 [8, 128, 128], P('head')
The draws below stay inside these ranges and needn't reach their ends.
All inputs are finite; a program needn't handle non-finite values.
Results may differ from the reference program's by a relative error of at most 0.00019.
Values sent between devices are 32-bit elements; how exact they have to be, the bound alone decides.
A program may use at most 64 MiB of HBM per device.

```python
import jax
import jax.numpy as jnp
from jax import lax

HEADS = 64
KV = 8
DH = 128
FEAT = 128
TOKENS = 4096


def paired_draw(key):
    seeded = jax.random.fold_in(key, 7321)
    key_one, key_two = jax.random.split(seeded, 2)
    query_vals = jnp.clip(jax.random.normal(key_one, (TOKENS, HEADS, DH), jnp.float32), -6.0, 6.0)
    key_vals = jnp.clip(jax.random.normal(key_two, (TOKENS, KV, DH), jnp.float32), -6.0, 6.0)
    return (query_vals.reshape(TOKENS, HEADS * DH), key_vals.reshape(TOKENS, KV * DH))


def draw_queries(key, part):
    return paired_draw(key)[0]


def draw_key_heads(key, part):
    return paired_draw(key)[1]


def steps_of(key, extent, pieces, least, largest):
    loudness = 1.0
    for axis_at, parts in pieces:
        heights = jax.random.uniform(jax.random.fold_in(jax.random.fold_in(key, 6), axis_at), (parts,), jnp.float32, least / len(pieces), largest / len(pieces))
        loudness = loudness * jnp.repeat(jnp.exp(heights), extent[axis_at] // parts).reshape((-1,) + (1,) * (len(extent) - 1 - axis_at))
    return loudness


def scatter_about(stream_key, extent, scale, bound, cuts=(), kind=jnp.bfloat16):
    result = scale * jax.random.normal(stream_key, extent, jnp.float32)
    if cuts:
        result = result * steps_of(stream_key, extent, cuts, -0.22, 0.18)
    return jnp.clip(result, -bound, bound).astype(kind)


def setup_inputs(seed: int = 0) -> dict:
    streams_of = jax.random.split(jax.random.key(seed), 6)
    queries = draw_queries(jax.random.fold_in(streams_of[5], 71), 0)
    key_heads = draw_key_heads(jax.random.fold_in(streams_of[5], 71), 0)
    value_heads = scatter_about(streams_of[2], (TOKENS, KV * DH), 1.0, 6.0, ((0, 16), (1, 8)), jnp.float32)
    query_map = scatter_about(streams_of[3], (HEADS, DH, FEAT), DH ** -0.5, 0.5, ((0, 8),), jnp.float32)
    key_map = scatter_about(streams_of[4], (KV, DH, FEAT), DH ** -0.5, 0.5, ((0, 8),), jnp.float32)
    return {"queries": queries, "key_heads": key_heads, "value_heads": value_heads, "query_map": query_map, "key_map": key_map}


HIGHEST = lax.Precision.HIGHEST
NEGATIVE = -1e+30
EPSILON = 1e-06

def head_grads(operands):
    query_head, key_head, value_head, query_weight, key_weight = operands
    positions = jnp.arange(TOKENS)
    causal = positions[:, None] >= positions[None, :]
    scores = jnp.dot(query_head, key_head.T, precision=HIGHEST) * DH ** (-0.5)
    masked = jnp.where(causal, scores, NEGATIVE)
    row_top = lax.optimization_barrier(jnp.max(masked, axis=1, keepdims=True))
    weights = jnp.where(causal, jnp.exp(masked - row_top), 0.0)
    teacher = jnp.dot(weights, value_head, precision=HIGHEST) / lax.optimization_barrier(jnp.sum(weights, axis=1, keepdims=True))

    def loss_of(query_map_head, key_map_head):
        query_feat = jax.nn.softplus(jnp.dot(query_head, query_map_head, precision=HIGHEST))
        key_feat = jax.nn.softplus(jnp.dot(key_head, key_map_head, precision=HIGHEST))
        kernel = jnp.where(causal, jnp.dot(query_feat, key_feat.T, precision=HIGHEST), 0.0)
        student = jnp.dot(kernel, value_head, precision=HIGHEST) / lax.optimization_barrier(jnp.sum(kernel, axis=1, keepdims=True))
        return 0.5 * jnp.sum((student - teacher) ** 2)
    return jax.grad(loss_of, argnums=(0, 1))(query_weight, key_weight)

def reference(queries, key_heads, value_heads, query_map, key_map):
    group_size = HEADS // KV
    query_split = queries.reshape(TOKENS, HEADS, DH).transpose(1, 0, 2)
    key_split = key_heads.reshape(TOKENS, KV, DH).transpose(1, 0, 2)
    value_split = value_heads.reshape(TOKENS, KV, DH).transpose(1, 0, 2)
    key_repeat = jnp.repeat(key_split, group_size, axis=0)
    value_repeat = jnp.repeat(value_split, group_size, axis=0)
    map_repeat = jnp.repeat(key_map, group_size, axis=0)
    grad_query, grad_key_heads = lax.map(head_grads, (query_split, key_repeat, value_repeat, query_map, map_repeat))
    grad_key = lax.optimization_barrier(jnp.sum(grad_key_heads.reshape(KV, group_size, DH, FEAT), axis=1))
    mean_square = (jnp.sum(grad_query * grad_query) + jnp.sum(grad_key * grad_key)) / ((HEADS + KV) * DH * FEAT)
    factor = 1.0 / jnp.sqrt(mean_square + EPSILON)
    return (grad_query * factor, grad_key * factor)
```

```python
import math

import jax
import jax.numpy as jnp
from jax import lax
from jax.experimental import pallas as pl
from jax.experimental.pallas import tpu as pltpu
from jax.sharding import PartitionSpec as P

NEGATIVE = -1e30
EPSILON = 1e-06
F32 = jnp.float32
BF16 = jnp.bfloat16


def halves(x):
    hi = x.astype(BF16)
    return hi, (x - hi.astype(F32)).astype(BF16)


def pair(x):
    return jnp.concatenate(halves(x), axis=1)


def twice(x, axis):
    return jnp.concatenate([x, x], axis=axis)


def stacked(x):
    hi, lo = halves(x)
    return jnp.concatenate([hi, hi, lo, lo], axis=0)


def dot(a, b):
    return jnp.dot(a, b, preferred_element_type=F32)


def dot_rows(a, b):
    return lax.dot_general(a, b, (((0,), (0,)), ((), ())), preferred_element_type=F32)


def fold(x):
    w = x.shape[1] // 2
    return x[:, :w] + x[:, w:]


def quad(x):
    h = x.shape[0] // 2
    y = fold(x)
    return y[:h] + y[h:]


def softplus_and_slope(x):
    e = jnp.exp(-jnp.abs(x))
    soft = jnp.maximum(x, 0.0) + jnp.log1p(e)
    slope = jnp.where(x >= 0.0, 1.0, e) / (1.0 + e)
    return soft, slope


MESH = pl.DeviceIdType.MESH


class Messages:
    def __init__(self, send_sems, recv_sems):
        self.send_sems, self.recv_sems, self.all = send_sems, recv_sems, {}

    def make(self, name, ref, peer):
        at = len(self.all)
        self.all[name] = pltpu.make_async_remote_copy(
            src_ref=ref, dst_ref=ref, send_sem=self.send_sems.at[at], recv_sem=self.recv_sems.at[at],
            device_id={"seq": peer}, device_id_type=MESH,
        )

    def start(self, *names):
        for name in names:
            self.all[name].start()

    def arrived(self, *names):
        for name in names:
            self.all[name].wait_recv()

    def sent(self):
        for copy in self.all.values():
            copy.wait_send()


def kernel(q_ref, k_ref, v_ref, qmap_ref, kmap_ref, gq_ref, gk_ref,
           q4, k4t, v4, sgk, sstate, norm, acc, top, tot, num, den, feat, a4, sgq,
           kbuf, vbuf, grad, parts, mine, whole, squares, head_squares, seq_squares,
           kv_send, kv_recv, rs_send, rs_recv, ag_send, ag_recv, sq_send, sq_recv):
    heads, dh = qmap_ref.shape[0], qmap_ref.shape[1]
    tok = q_ref.shape[0]
    me = lax.axis_index("seq")
    my_head = lax.axis_index("head")
    n_seq, n_head = kbuf.shape[0], head_squares.shape[0] + 1
    side = math.isqrt(n_seq)
    my_x, my_z = me // side, lax.rem(me, side)

    def at(dx, dz):
        return lax.rem(my_x + dx + side, side) * side + lax.rem(my_z + dz + side, side)

    barrier = pltpu.get_barrier_semaphore()

    def greet_seq(k, _):
        pl.semaphore_signal(barrier, inc=1, device_id={"seq": lax.rem(me + k, n_seq)}, device_id_type=MESH)
        return 0

    def greet_head(k, _):
        pl.semaphore_signal(barrier, inc=1, device_id={"head": lax.rem(my_head + k, n_head)}, device_id_type=MESH)
        return 0

    lax.fori_loop(1, n_seq, greet_seq, 0)
    lax.fori_loop(1, n_head, greet_head, 0)
    kbuf[me] = k_ref[...]
    vbuf[me] = v_ref[...]
    pl.semaphore_wait(barrier, n_seq + n_head - 2)

    half = tok // 2
    msgs = Messages(kv_send, kv_recv)
    for tag, buf, flip in (("k", kbuf, False), ("v", vbuf, True)):
        def place(a, b):
            return at(b, a) if flip else at(a, b)

        def route(name, a, b, first):
            up = place(1, 0) if first else place(0, 1)
            down = place(-1, 0) if first else place(0, -1)
            msgs.make(tag + name + "+", buf.at[place(a, b)], up)
            msgs.make(tag + name + "-", buf.at[place(a, b)], down)
            pa, pb, na, nb = (a - 1, b, a + 1, b) if first else (a, b - 1, a, b + 1)
            msgs.make(tag + name + "++", buf.at[place(pa, pb), pl.ds(0, half)], up)
            msgs.make(tag + name + "--", buf.at[place(na, nb), pl.ds(half, half)], down)

        route("1", 0, 0, True)
        for name, a in (("a", 0), ("b", -1), ("c", 1), ("d", 2)):
            route(name, a, 0, False)

    def both(*names):
        return [t + x for t in "kv" for x in names]

    scale = dh ** -0.5 * math.log2(math.e)
    rows = lax.broadcasted_iota(jnp.int32, (tok, tok), 0)
    cols = lax.broadcasted_iota(jnp.int32, (tok, tok), 1)
    causal = rows >= cols
    kmap2 = twice(pair(kmap_ref[0]), 0)

    def prepare(j):
        k, v = kbuf[j], vbuf[j]
        k4t[j] = stacked(k.T * scale)
        v2 = pair(v)
        v4[j] = twice(v2, 0)
        act = fold(dot(pair(k), kmap2))
        b, slope = softplus_and_slope(act)
        sgk[j] = slope
        return b, v2

    def prefix(j, _):
        b, v2 = prepare(j)
        sstate[...] += quad(dot_rows(pair(b), v2))
        norm[...] += jnp.sum(b, axis=0, keepdims=True)
        return 0

    def attend(h, j, first):
        s = dot(q4[h], k4t[j])
        if first:
            s = jnp.where(causal, s, NEGATIVE)
        new = jnp.max(s, axis=1, keepdims=True)
        if first:
            new = jnp.broadcast_to(new, (tok, dh))
        else:
            old = top[h]
            new = jnp.maximum(old, new)
            alpha = jnp.exp2(old - new)
        p = jnp.exp2(s - twice(new, 1))
        o = fold(dot(pair(p), v4[j]))
        if first:
            tot[h] = fold(p)
            acc[h] = o
        else:
            tot[h] = tot[h] * alpha + fold(p)
            acc[h] = acc[h] * alpha + o
        top[h] = new

    msgs.start(*both("1+", "1-", "a+", "a-"))
    sstate[...] = jnp.zeros_like(sstate)
    norm[...] = jnp.zeros_like(norm)
    b_own, v2_own = prepare(me)
    v_own = v_ref[...]
    b4 = twice(pair(b_own), 0)
    b4t = stacked(b_own.T)
    v4t = stacked(v_own.T)

    def before(h, _):
        q2 = pair(q_ref[:, pl.ds(pl.multiple_of(h * dh, dh), dh)])
        q4[h] = twice(q2, 1)
        act = fold(dot(q2, twice(pair(qmap_ref[h]), 0)))
        a, slope = softplus_and_slope(act)
        sgq[h] = slope
        feat[h] = a
        a4[h] = twice(pair(a), 1)
        ker = jnp.where(causal, dot(a4[h], b4t), 0.0)
        den[h] = jnp.broadcast_to(jnp.sum(ker, axis=1, keepdims=True), (tok, dh))
        num[h] = fold(dot(pair(ker), v4[me]))
        attend(h, me, True)
        return 0

    lax.fori_loop(0, heads, before, 0)

    def block(j):
        @pl.when(j < me)
        def _():
            prefix(j, 0)

            def two(h, _):
                attend(2 * h, j, False)
                attend(2 * h + 1, j, False)
                return 0

            lax.fori_loop(0, heads // 2, two, 0)

    def near(t, _):
        step = 2 * lax.rem(t, 2) - 1
        block(at(step * (1 - t // 2), step * (t // 2)))
        return 0

    def across(t, _):
        block(at(2 * t, 2 * (1 - t)))
        return 0

    def corner(t, _):
        block(at(2 * (t // 2) - 1, 2 * lax.rem(t, 2) - 1))
        return 0

    def knight(t, _):
        step = 2 * lax.rem(t, 2) - 1
        block(at(step * (1 - t // 2) + 2 * (t // 2), 2 * (1 - t // 2) + step * (t // 2)))
        return 0

    msgs.arrived(*both("1+", "1-"))
    msgs.start(*both("1++", "1--", "b+", "b-", "c+", "c-"))
    msgs.arrived(*both("a+", "a-"))
    msgs.start(*both("a++", "a--"))
    lax.fori_loop(0, 4, near, 0)
    msgs.arrived(*both("1++", "1--"))
    msgs.start(*both("d+", "d-"))
    msgs.arrived(*both("a++", "a--"))
    lax.fori_loop(0, 2, across, 0)
    msgs.arrived(*both("b+", "b-", "c+", "c-"))
    msgs.start(*both("b++", "b--", "c++", "c--"))
    lax.fori_loop(0, 4, corner, 0)
    msgs.arrived(*both("d+", "d-"))
    msgs.start(*both("d++", "d--"))
    msgs.arrived(*both("b++", "b--", "c++", "c--"))
    lax.fori_loop(0, 4, knight, 0)
    msgs.arrived(*both("d++", "d--"))
    block(at(2, 2))

    state2 = twice(pair(sstate[...]), 0)
    state2t = twice(pair(sstate[...].T), 0)
    norm_row = norm[...]

    def after(h, carry):
        adj, adjn, gkd = carry
        a = feat[h]
        a2 = a4[h, :, : 2 * dh]
        q2 = q4[h, :, : 2 * dh]
        rden = 1.0 / (den[h] + jnp.sum(a * norm_row, axis=1, keepdims=True))
        student = (num[h] + fold(dot(a2, state2))) * rden
        teacher = acc[h] / jnp.sum(tot[h], axis=1, keepdims=True)
        mis = student - teacher
        gn = mis * rden
        gd = -jnp.sum(gn * student, axis=1, keepdims=True)
        gn2 = pair(gn)
        coup = jnp.where(causal, dot(twice(gn2, 1), v4t) + gd, 0.0)
        c2 = pair(coup)
        gq = fold(dot(c2, b4)) + fold(dot(gn2, state2t)) + gd * norm_row
        grad[h] = quad(dot_rows(q2, pair(gq * sgq[h])))
        adj = adj + quad(dot_rows(a2, gn2))
        adjn = adjn + jnp.sum(a * gd, axis=0, keepdims=True)
        gkd = gkd + quad(dot_rows(c2, a2))
        return adj, adjn, gkd

    width = dh // n_seq
    groups = ((0, heads // 2), (heads // 2, heads // 2), (heads, 1))

    def rows_of(d):
        return pl.ds(pl.multiple_of(d * width, width), width)

    def scatter(g):
        first, count = groups[g]

        def send(k, _):
            peer = lax.rem(me + k, n_seq)
            pltpu.make_async_remote_copy(
                src_ref=grad.at[pl.ds(first, count), rows_of(peer)],
                dst_ref=parts.at[k - 1, pl.ds(first, count)],
                send_sem=rs_send.at[g], recv_sem=rs_recv.at[g],
                device_id={"seq": peer}, device_id_type=MESH,
            ).start()
            return 0

        lax.fori_loop(1, n_seq, send, 0)

    def all_of(ref, sem):
        pltpu.make_async_copy(ref, ref, sem).wait()

    def gather(g):
        first, count = groups[g]
        span = pl.ds(first, count)
        all_of(parts.at[:, span], rs_recv.at[g])
        total = grad[span, rows_of(me)]
        for k in range(n_seq - 1):
            total = total + parts[k, span]
        mine[span] = total
        whole[span, rows_of(me)] = total

        def send(k, _):
            pltpu.make_async_remote_copy(
                src_ref=mine.at[span],
                dst_ref=whole.at[span, rows_of(me)],
                send_sem=ag_send.at[g], recv_sem=ag_recv.at[g],
                device_id={"seq": lax.rem(me + k, n_seq)}, device_id_type=MESH,
            ).start()
            return 0

        lax.fori_loop(1, n_seq, send, 0)
        return jnp.sum(total * total, axis=0)

    carry = (jnp.zeros((dh, dh), F32), jnp.zeros((1, dh), F32), jnp.zeros((tok, dh), F32))
    carry = lax.fori_loop(0, heads // 2, after, carry)
    scatter(0)
    adj, adjn, gkd = lax.fori_loop(heads // 2, heads, after, carry)
    scatter(1)
    adjt2 = twice(pair(adj.T), 0)

    grad[heads] = quad(dot_rows(pair(k_ref[...]), pair(gkd * sgk[me])))

    def later(j, _):
        g = fold(dot(v4[j, :tok], adjt2)) + adjn
        grad[heads] += quad(dot_rows(pair(kbuf[j]), pair(g * sgk[j])))
        return 0

    lax.fori_loop(0, me, later, 0)
    scatter(2)
    squares[0] = gather(0) + gather(1) + gather(2)

    def send_head(k, _):
        pltpu.make_async_remote_copy(
            src_ref=squares.at[0], dst_ref=head_squares.at[k - 1],
            send_sem=sq_send.at[0], recv_sem=sq_recv.at[0],
            device_id={"head": lax.rem(my_head + k, n_head)}, device_id_type=MESH,
        ).start()
        return 0

    def send_seq(k, _):
        pltpu.make_async_remote_copy(
            src_ref=squares.at[1], dst_ref=seq_squares.at[k - 1],
            send_sem=sq_send.at[1], recv_sem=sq_recv.at[1],
            device_id={"seq": lax.rem(me + k, n_seq)}, device_id_type=MESH,
        ).start()
        return 0

    lax.fori_loop(1, n_head, send_head, 0)
    all_of(head_squares, sq_recv.at[0])
    squares[1] = squares[0] + jnp.sum(head_squares[...], axis=0)
    lax.fori_loop(1, n_seq, send_seq, 0)
    all_of(seq_squares, sq_recv.at[1])
    square = jnp.sum(squares[1] + jnp.sum(seq_squares[...], axis=0))
    size = (heads + 1) * n_head * dh * grad.shape[2]
    factor = 1.0 / jnp.sqrt(jnp.broadcast_to(square / size + EPSILON, (1, dh)))
    for g in range(3):
        first, count = groups[g]
        all_of(parts.at[:, pl.ds(first, count)], ag_recv.at[g])
    gq_ref[...] = whole[pl.ds(0, heads)] * factor
    gk_ref[...] = whole[pl.ds(heads, 1)] * factor

    msgs.sent()
    for g in range(3):
        first, count = groups[g]
        all_of(parts.at[:, pl.ds(first, count)], rs_send.at[g])
        all_of(parts.at[:, pl.ds(first, count)], ag_send.at[g])
    all_of(head_squares, sq_send.at[0])
    all_of(seq_squares, sq_send.at[1])


def on_device(queries, key_heads, value_heads, query_map, key_map):
    tok = queries.shape[0]
    heads, dh, feats = query_map.shape
    n = lax.axis_size("seq")
    return pl.pallas_call(
        kernel,
        out_shape=(jax.ShapeDtypeStruct((heads, dh, feats), F32), jax.ShapeDtypeStruct((1, dh, feats), F32)),
        in_specs=[pl.BlockSpec(memory_space=pltpu.VMEM)] * 5,
        out_specs=(pl.BlockSpec(memory_space=pltpu.VMEM),) * 2,
        scratch_shapes=[
            pltpu.VMEM((heads, tok, 4 * dh), BF16),
            pltpu.VMEM((n, 4 * dh, tok), BF16),
            pltpu.VMEM((n, 2 * tok, 2 * dh), BF16),
            pltpu.VMEM((n, tok, feats), F32),
            pltpu.VMEM((feats, dh), F32),
            pltpu.VMEM((1, feats), F32),
            pltpu.VMEM((heads, tok, dh), F32),
            pltpu.VMEM((heads, tok, dh), F32),
            pltpu.VMEM((heads, tok, dh), F32),
            pltpu.VMEM((heads, tok, dh), F32),
            pltpu.VMEM((heads, tok, dh), F32),
            pltpu.VMEM((heads, tok, feats), F32),
            pltpu.VMEM((heads, tok, 4 * feats), BF16),
            pltpu.VMEM((heads, tok, feats), F32),
            pltpu.VMEM((n, tok, dh), F32),
            pltpu.VMEM((n, tok, dh), F32),
            pltpu.VMEM((heads + 1, dh, feats), F32),
            pltpu.VMEM((n - 1, heads + 1, dh // n, feats), F32),
            pltpu.VMEM((heads + 1, dh // n, feats), F32),
            pltpu.VMEM((heads + 1, dh, feats), F32),
            pltpu.VMEM((2, dh // n, feats), F32),
            pltpu.VMEM((lax.axis_size("head") - 1, dh // n, feats), F32),
            pltpu.VMEM((n - 1, dh // n, feats), F32),
            pltpu.SemaphoreType.DMA((40,)),
            pltpu.SemaphoreType.DMA((40,)),
        ] + [pltpu.SemaphoreType.DMA((3,))] * 4 + [pltpu.SemaphoreType.DMA((2,))] * 2,
        compiler_params=pltpu.CompilerParams(vmem_limit_bytes=56 * 2**20, collective_id=0, has_side_effects=True),
    )(queries, key_heads, value_heads, query_map, key_map)


def solution(mesh):
    return jax.shard_map(
        on_device,
        mesh=mesh,
        in_specs=(P("seq", "head"), P("seq", "head"), P("seq", "head"), P("head"), P("head")),
        out_specs=(P("head"), P("head")),
        check_vma=False,
    )
```

```python
import math

import jax
import jax.numpy as jnp
from jax import lax
from jax.experimental import pallas as pl
from jax.experimental.pallas import tpu as pltpu
from jax.sharding import PartitionSpec as P

NEGATIVE = -1e30
EPSILON = 1e-06
F32 = jnp.float32
BF16 = jnp.bfloat16


def halves(x):
    hi = x.astype(BF16)
    return hi, (x - hi.astype(F32)).astype(BF16)


def pair(x):
    return jnp.concatenate(halves(x), axis=1)


def twice(x, axis):
    return jnp.concatenate([x, x], axis=axis)


def stacked(x):
    hi, lo = halves(x)
    return jnp.concatenate([hi, hi, lo, lo], axis=0)


def dot(a, b):
    return jnp.dot(a, b, preferred_element_type=F32)


def dot_rows(a, b):
    return lax.dot_general(a, b, (((0,), (0,)), ((), ())), preferred_element_type=F32)


def fold(x):
    w = x.shape[1] // 2
    return x[:, :w] + x[:, w:]


def quad(x):
    h = x.shape[0] // 2
    y = fold(x)
    return y[:h] + y[h:]


def softplus_and_slope(x):
    e = jnp.exp(-jnp.abs(x))
    soft = jnp.maximum(x, 0.0) + jnp.log1p(e)
    slope = jnp.where(x >= 0.0, 1.0, e) / (1.0 + e)
    return soft, slope


MESH = pl.DeviceIdType.MESH


class Messages:
    def __init__(self, send_sems, recv_sems):
        self.send_sems, self.recv_sems, self.all = send_sems, recv_sems, {}

    def make(self, name, ref, peer):
        at = len(self.all)
        self.all[name] = pltpu.make_async_remote_copy(
            src_ref=ref, dst_ref=ref, send_sem=self.send_sems.at[at], recv_sem=self.recv_sems.at[at],
            device_id={"seq": peer}, device_id_type=MESH,
        )

    def start(self, *names):
        for name in names:
            self.all[name].start()

    def arrived(self, *names):
        for name in names:
            self.all[name].wait_recv()

    def sent(self):
        for copy in self.all.values():
            copy.wait_send()


def kernel(q_ref, k_ref, v_ref, qmap_ref, kmap_ref, gq_ref, gk_ref,
           q4, k4t, v4, k2t, sgk, state, norm, acc, top, tot, num, den, feat, a4, sgq, b4, b4t, v4t, adjs, adjt2, adjns, gkds,
           kbuf, vbuf, qbuf, grad, parts, mine, whole, squares, head_squares, seq_squares,
           kv_send, kv_recv, q_send, q_recv, rs_send, rs_recv, ag_send, ag_recv, sq_send, sq_recv):
    heads, dh = qmap_ref.shape[0], qmap_ref.shape[1]
    tok = q_ref.shape[0]
    me = lax.axis_index("seq")
    my_head = lax.axis_index("head")
    n_seq, n_head = kbuf.shape[0], head_squares.shape[0] + 1
    side = math.isqrt(n_seq)
    my_x, my_z = me // side, lax.rem(me, side)
    given = qbuf.shape[1] // dh
    kept = heads - given
    far = n_seq - 1 - me
    early = me < n_seq // 2
    main = list(range(kept))
    rest = list(range(kept, heads))
    guest = list(range(heads, heads + given))

    def at(dx, dz):
        return lax.rem(my_x + dx + side, side) * side + lax.rem(my_z + dz + side, side)

    barrier = pltpu.get_barrier_semaphore()
    for peer in (at(1, 0), at(-1, 0), at(0, 1), at(0, -1), far):
        pl.semaphore_signal(barrier, inc=1, device_id={"seq": peer}, device_id_type=MESH)

    def greet_head(k, _):
        pl.semaphore_signal(barrier, inc=1, device_id={"head": lax.rem(my_head + k, n_head)}, device_id_type=MESH)
        return 0

    lax.fori_loop(1, n_head, greet_head, 0)
    kbuf[me] = k_ref[...]
    vbuf[me] = v_ref[...]

    half = tok // 2
    msgs = Messages(kv_send, kv_recv)
    for tag, buf, flip in (("k", kbuf, False), ("v", vbuf, True)):
        def place(a, b):
            return at(b, a) if flip else at(a, b)

        def route(name, a, b, first):
            up = place(1, 0) if first else place(0, 1)
            down = place(-1, 0) if first else place(0, -1)
            msgs.make(tag + name + "+", buf.at[place(a, b)], up)
            msgs.make(tag + name + "-", buf.at[place(a, b)], down)
            pa, pb, na, nb = (a - 1, b, a + 1, b) if first else (a, b - 1, a, b + 1)
            msgs.make(tag + name + "++", buf.at[place(pa, pb), pl.ds(0, half)], up)
            msgs.make(tag + name + "--", buf.at[place(na, nb), pl.ds(half, half)], down)

        route("1", 0, 0, True)
        for name, a in (("a", 0), ("b", -1), ("c", 1), ("d", 2)):
            route(name, a, 0, False)

    def both(*names):
        return [t + x for t in "kv" for x in names]

    query_copy = pltpu.make_async_remote_copy(
        src_ref=q_ref.at[:, pl.ds(kept * dh, given * dh)], dst_ref=qbuf,
        send_sem=q_send.at[0], recv_sem=q_recv.at[0], device_id={"seq": far}, device_id_type=MESH,
    )

    scale = dh ** -0.5 * math.log2(math.e)
    rows = lax.broadcasted_iota(jnp.int32, (tok, tok), 0)
    cols = lax.broadcasted_iota(jnp.int32, (tok, tok), 1)
    causal = rows >= cols
    kmap2 = twice(pair(kmap_ref[0]), 0)

    def prepare(j):
        k, v = kbuf[j], vbuf[j]
        kt = k.T
        keys = stacked(kt * scale)
        k4t[j] = keys
        k2t[j] = jnp.concatenate(halves(kt), axis=0)
        v2 = pair(v)
        values = twice(v2, 0)
        v4[j] = values
        b, slope = softplus_and_slope(fold(dot(pair(k), kmap2)))
        sgk[j] = slope
        return keys, values, b, v2

    def diagonal(n, b, v):
        b4[n] = twice(pair(b), 0)
        b4t[n] = stacked(b.T)
        v4t[n] = stacked(v.T)

    def attend(group, keys, values, masked=False, fresh=False):
        scores = [dot(q4[h], keys) for h in group]
        if not fresh:
            before = [(top[h], tot[h], acc[h]) for h in group]
        found = []
        for i, s in enumerate(scores):
            if masked:
                s = jnp.where(causal, s, NEGATIVE)
            new = jnp.max(s, axis=1, keepdims=True)
            if fresh:
                new = jnp.broadcast_to(new, (tok, dh))
            else:
                new = jnp.maximum(before[i][0], new)
                alpha = jnp.exp2(before[i][0] - new)
            p = jnp.exp2(s - twice(new, 1))
            o = fold(dot(pair(p), values))
            t = fold(p)
            if not fresh:
                t = before[i][1] * alpha + t
                o = before[i][2] * alpha + o
            found.append((new, t, o))
        for h, (new, t, o) in zip(group, found):
            top[h], tot[h], acc[h] = new, t, o

    def load_queries(slots, source):
        for h, q in zip(slots, source):
            q4[h] = twice(pair(q), 1)

    def before(slots, names, n, j, fresh):
        values = v4[j]
        acts = [fold(dot(q4[h, :, : 2 * dh], twice(pair(qmap_ref[m]), 0))) for h, m in zip(slots, names)]
        soft = [softplus_and_slope(act) for act in acts]
        a4s = [twice(pair(a), 1) for a, _ in soft]
        for h, (a, slope), four in zip(slots, soft, a4s):
            feat[h], sgq[h], a4[h] = a, slope, four
        kers = [jnp.where(causal, dot(four, b4t[n]), 0.0) for four in a4s]
        nums = [fold(dot(pair(ker), values)) for ker in kers]
        for h, ker, nm in zip(slots, kers, nums):
            den[h] = jnp.broadcast_to(jnp.sum(ker, axis=1, keepdims=True), (tok, dh))
            num[h] = nm
        attend(slots, k4t[j], values, masked=True, fresh=fresh)

    def own_queries(slots):
        return [q_ref[:, h * dh : (h + 1) * dh] for h in slots]

    state[...] = jnp.zeros_like(state)
    norm[...] = jnp.zeros_like(norm)
    adjns[...] = jnp.zeros_like(adjns)
    adjt2[...] = jnp.zeros_like(adjt2)
    _, _, b_own, v2_own = prepare(me)
    diagonal(0, b_own, v_ref[...])
    state_own = quad(dot_rows(pair(b_own), v2_own))
    norm_own = jnp.sum(b_own, axis=0, keepdims=True)

    def add_state(n, s, b):
        state[n] += s
        norm[n] += b

    def begin(slots):
        load_queries(slots, own_queries(slots))
        before(slots, slots, 0, me, True)

    cut = kept // 2
    begin(main[:cut])
    pl.semaphore_wait(barrier, n_head + 4)
    msgs.start(*both("1+", "1-", "a+", "a-"))

    @pl.when(jnp.logical_not(early))
    def _():
        query_copy.start()

    begin(main[cut:])

    @pl.when(early)
    def _():
        begin(rest)
        add_state(1, state_own, norm_own)

    msgs.arrived(*both("1+", "1-"))
    msgs.start(*both("1++", "1--", "b+", "b-", "c+", "c-"))

    @pl.when(early)
    def _():
        query_copy.wait_recv()
        load_queries(guest, [qbuf[:, i * dh : (i + 1) * dh] for i in range(given)])
        for h in guest:
            top[h] = jnp.full((tok, dh), NEGATIVE, F32)
            tot[h] = jnp.zeros((tok, dh), F32)
            acc[h] = jnp.zeros((tok, dh), F32)
        attend(guest, k4t[me], v4[me])

    def block(j):
        @pl.when(j < me)
        def _():
            keys, values, b, v2 = prepare(j)
            attend(main, keys, values)
            s, c = quad(dot_rows(pair(b), v2)), jnp.sum(b, axis=0, keepdims=True)
            add_state(0, s, c)
            add_state(1, s, c)

            @pl.when(early)
            def _():
                attend(rest + guest, keys, values)

        @pl.when(jnp.logical_and(j > me, j <= far))
        def _():
            keys, values, b, v2 = prepare(j)

            @pl.when(j < far)
            def _():
                attend(guest, keys, values)
                add_state(1, quad(dot_rows(pair(b), v2)), jnp.sum(b, axis=0, keepdims=True))

            @pl.when(j == far)
            def _():
                diagonal(1, b, vbuf[j])
                before(guest, rest, 1, j, False)

    order = (
        (0, 3), (0, 1), (3, 0), (1, 0), (0, 2), (2, 0), (3, 3), (3, 1), (1, 3), (1, 1),
        (3, 2), (1, 2), (2, 3), (2, 1), (2, 2),
    )

    def step(t, _):
        @pl.when(t == 0)
        def _():
            msgs.arrived(*both("a+", "a-"))
            msgs.start(*both("a++", "a--"))

        @pl.when(t == 4)
        def _():
            msgs.arrived(*both("1++", "1--"))
            msgs.start(*both("d+", "d-"))
            msgs.arrived(*both("a++", "a--"))

        @pl.when(t == 6)
        def _():
            msgs.arrived(*both("b+", "b-", "c+", "c-"))
            msgs.start(*both("b++", "b--", "c++", "c--"))

        @pl.when(t == 10)
        def _():
            msgs.arrived(*both("d+", "d-"))
            msgs.start(*both("d++", "d--"))
            msgs.arrived(*both("b++", "b--", "c++", "c--"))

        @pl.when(t == 14)
        def _():
            msgs.arrived(*both("d++", "d--"))

        dx, dz = jnp.int32(0), jnp.int32(0)
        for i, (ox, oz) in enumerate(order):
            dx = jnp.where(t == i, ox, dx)
            dz = jnp.where(t == i, oz, dz)
        block(at(dx, dz))
        return 0

    lax.fori_loop(0, n_seq - 1, step, 0)

    def after(slots, n):
        state2 = twice(pair(state[n]), 0)
        state2t = twice(pair(state[n].T), 0)
        norm_row = norm[n]
        feats = [feat[h] for h in slots]
        a2s = [a4[h, :, : 2 * dh] for h in slots]
        inter = [fold(dot(a2, state2)) for a2 in a2s]
        gns, gds = [], []
        for h, a, more in zip(slots, feats, inter):
            rden = 1.0 / (den[h] + jnp.sum(a * norm_row, axis=1, keepdims=True))
            student = (num[h] + more) * rden
            teacher = acc[h] / jnp.sum(tot[h], axis=1, keepdims=True)
            gn = (student - teacher) * rden
            gns.append(pair(gn))
            gds.append(-jnp.sum(gn * student, axis=1, keepdims=True))
        coups = [dot(twice(gn2, 1), v4t[n]) for gn2 in gns]
        c2s = [pair(jnp.where(causal, c + gd, 0.0)) for c, gd in zip(coups, gds)]
        gqs = [
            fold(dot(c2, b4[n])) + fold(dot(gn2, state2t)) + gd * norm_row
            for c2, gn2, gd in zip(c2s, gns, gds)
        ]
        grads = [quad(dot_rows(q4[h, :, : 2 * dh], pair(g * sgq[h]))) for h, g in zip(slots, gqs)]
        adj = sum(quad(dot_rows(a2, gn2)) for a2, gn2 in zip(a2s, gns))
        adjn = sum(jnp.sum(a * gd, axis=0, keepdims=True) for a, gd in zip(feats, gds))
        gkd = sum(quad(dot_rows(c2, a2)) for c2, a2 in zip(c2s, a2s))
        return grads, adj, adjn, gkd

    width = dh // n_seq
    groups = ((0, cut), (cut, heads - cut), (heads, 1))

    def rows_of(d):
        return pl.ds(pl.multiple_of(d * width, width), width)

    def scatter(g):
        first, count = groups[g]

        def send(k, _):
            peer = lax.rem(me + k, n_seq)
            pltpu.make_async_remote_copy(
                src_ref=grad.at[pl.ds(first, count), rows_of(peer)],
                dst_ref=parts.at[k - 1, pl.ds(first, count)],
                send_sem=rs_send.at[g], recv_sem=rs_recv.at[g],
                device_id={"seq": peer}, device_id_type=MESH,
            ).start()
            return 0

        lax.fori_loop(1, n_seq, send, 0)

    def all_of(ref, sem):
        pltpu.make_async_copy(ref, ref, sem).wait()

    def gather(g):
        first, count = groups[g]
        span = pl.ds(first, count)
        all_of(parts.at[:, span], rs_recv.at[g])
        total = grad[span, rows_of(me)]
        for k in range(n_seq - 1):
            total = total + parts[k, span]
        mine[span] = total
        whole[span, rows_of(me)] = total

        def send(k, _):
            pltpu.make_async_remote_copy(
                src_ref=mine.at[span],
                dst_ref=whole.at[span, rows_of(me)],
                send_sem=ag_send.at[g], recv_sem=ag_recv.at[g],
                device_id={"seq": lax.rem(me + k, n_seq)}, device_id_type=MESH,
            ).start()
            return 0

        lax.fori_loop(1, n_seq, send, 0)
        return jnp.sum(total * total, axis=0)

    def keep(grads, slots):
        for h, g in zip(slots, grads):
            grad[h] = g

    grads, adj, adjn, gkd = after(main[:cut], 0)
    keep(grads, main[:cut])
    scatter(0)
    grads, adj_b, adjn_b, gkd_b = after(main[cut:], 0)
    keep(grads, main[cut:])
    adjs[...] = adj + adj_b
    adjns[0] = adjn + adjn_b
    gkds[0] = gkd + gkd_b

    @pl.when(early)
    def _():
        grads, adj, adjn, gkd = after(rest, 0)
        guests, adj_g, adjn_g, gkd_g = after(guest, 1)
        keep([u + w for u, w in zip(grads, guests)], rest)
        adjs[...] += adj + adj_g
        adjns[0] += adjn + adjn_g
        gkds[0] += gkd
        gkds[1] = gkd_g
        adjt2[1] = twice(pair(adj_g.T), 0)
        adjns[1] = adjn_g

    @pl.when(jnp.logical_not(early))
    def _():
        for h in rest:
            grad[h] = jnp.zeros((dh, dh), F32)

    scatter(1)

    adjt2[0] = twice(pair(adjs[...].T), 0)
    limit = jnp.where(early, far, me)

    def diagonal_grad(n, j):
        return quad(dot(k2t[j], pair(gkds[n] * sgk[j])))

    grad[heads] = diagonal_grad(0, me)

    @pl.when(early)
    def _():
        grad[heads] += diagonal_grad(1, far)

    batch = 4

    def later(c, _):
        js = [batch * c + i for i in range(batch)]
        which = [jnp.where(j < me, 0, 1) for j in js]
        outs = [fold(dot(v4[j, :tok], adjt2[w])) + adjns[w] for j, w in zip(js, which)]
        dks = [pair(jnp.where(j < limit, g * sgk[j], 0.0)) for j, g in zip(js, outs)]
        grad[heads] += quad(sum(dot(k2t[j], dk) for j, dk in zip(js, dks)))
        return 0

    lax.fori_loop(0, (limit + batch - 1) // batch, later, 0)
    scatter(2)
    squares[0] = gather(0) + gather(1)
    squares[0] += gather(2)

    def send_head(k, _):
        pltpu.make_async_remote_copy(
            src_ref=squares.at[0], dst_ref=head_squares.at[k - 1],
            send_sem=sq_send.at[0], recv_sem=sq_recv.at[0],
            device_id={"head": lax.rem(my_head + k, n_head)}, device_id_type=MESH,
        ).start()
        return 0

    def send_seq(k, _):
        pltpu.make_async_remote_copy(
            src_ref=squares.at[1], dst_ref=seq_squares.at[k - 1],
            send_sem=sq_send.at[1], recv_sem=sq_recv.at[1],
            device_id={"seq": lax.rem(me + k, n_seq)}, device_id_type=MESH,
        ).start()
        return 0

    lax.fori_loop(1, n_head, send_head, 0)
    all_of(head_squares, sq_recv.at[0])
    squares[1] = squares[0] + jnp.sum(head_squares[...], axis=0)
    lax.fori_loop(1, n_seq, send_seq, 0)
    all_of(seq_squares, sq_recv.at[1])
    square = jnp.sum(squares[1] + jnp.sum(seq_squares[...], axis=0))
    size = (heads + 1) * n_head * dh * grad.shape[2]
    factor = 1.0 / jnp.sqrt(jnp.broadcast_to(square / size + EPSILON, (1, dh)))
    for g in range(3):
        first, count = groups[g]
        all_of(parts.at[:, pl.ds(first, count)], ag_recv.at[g])
    gq_ref[...] = whole[pl.ds(0, heads)] * factor
    gk_ref[...] = whole[pl.ds(heads, 1)] * factor

    msgs.sent()

    @pl.when(jnp.logical_not(early))
    def _():
        query_copy.wait_send()

    for g in range(3):
        first, count = groups[g]
        all_of(parts.at[:, pl.ds(first, count)], rs_send.at[g])
        all_of(parts.at[:, pl.ds(first, count)], ag_send.at[g])
    all_of(head_squares, sq_send.at[0])
    all_of(seq_squares, sq_send.at[1])


def on_device(queries, key_heads, value_heads, query_map, key_map):
    tok = queries.shape[0]
    heads, dh, feats = query_map.shape
    n = lax.axis_size("seq")
    given = heads // 4
    slots = heads + given
    return pl.pallas_call(
        kernel,
        out_shape=(jax.ShapeDtypeStruct((heads, dh, feats), F32), jax.ShapeDtypeStruct((1, dh, feats), F32)),
        in_specs=[pl.BlockSpec(memory_space=pltpu.VMEM)] * 5,
        out_specs=(pl.BlockSpec(memory_space=pltpu.VMEM),) * 2,
        scratch_shapes=[
            pltpu.VMEM((slots, tok, 4 * dh), BF16),
            pltpu.VMEM((n, 4 * dh, tok), BF16),
            pltpu.VMEM((n, 2 * tok, 2 * dh), BF16),
            pltpu.VMEM((n, 2 * dh, tok), BF16),
            pltpu.VMEM((n, tok, feats), F32),
            pltpu.VMEM((2, feats, dh), F32),
            pltpu.VMEM((2, 1, feats), F32),
        ] + [pltpu.VMEM((slots, tok, dh), F32)] * 6 + [
            pltpu.VMEM((slots, tok, 4 * feats), BF16),
            pltpu.VMEM((slots, tok, feats), F32),
            pltpu.VMEM((2, 2 * tok, 2 * feats), BF16),
            pltpu.VMEM((2, 4 * feats, tok), BF16),
            pltpu.VMEM((2, 4 * dh, tok), BF16),
            pltpu.VMEM((feats, dh), F32),
            pltpu.VMEM((2, 2 * dh, 2 * feats), BF16),
            pltpu.VMEM((2, 1, feats), F32),
            pltpu.VMEM((2, tok, feats), F32),
            pltpu.VMEM((n, tok, dh), F32),
            pltpu.VMEM((n, tok, dh), F32),
            pltpu.VMEM((tok, given * dh), F32),
            pltpu.VMEM((heads + 1, dh, feats), F32),
            pltpu.VMEM((n - 1, heads + 1, dh // n, feats), F32),
            pltpu.VMEM((heads + 1, dh // n, feats), F32),
            pltpu.VMEM((heads + 1, dh, feats), F32),
            pltpu.VMEM((2, dh // n, feats), F32),
            pltpu.VMEM((lax.axis_size("head") - 1, dh // n, feats), F32),
            pltpu.VMEM((n - 1, dh // n, feats), F32),
            pltpu.SemaphoreType.DMA((40,)),
            pltpu.SemaphoreType.DMA((40,)),
            pltpu.SemaphoreType.DMA((1,)),
            pltpu.SemaphoreType.DMA((1,)),
        ] + [pltpu.SemaphoreType.DMA((3,))] * 4 + [pltpu.SemaphoreType.DMA((2,))] * 2,
        compiler_params=pltpu.CompilerParams(vmem_limit_bytes=56 * 2**20, collective_id=0, has_side_effects=True),
    )(queries, key_heads, value_heads, query_map, key_map)


def solution(mesh):
    return jax.shard_map(
        on_device,
        mesh=mesh,
        in_specs=(P("seq", "head"), P("seq", "head"), P("seq", "head"), P("head"), P("head")),
        out_specs=(P("head"), P("head")),
        check_vma=False,
    )
```

```python
import math

import jax
import jax.numpy as jnp
from jax import lax
from jax.experimental import pallas as pl
from jax.experimental.pallas import tpu as pltpu
from jax.sharding import PartitionSpec as P

NEGATIVE = -1e30
EPSILON = 1e-06
F32 = jnp.float32
BF16 = jnp.bfloat16


def halves(x):
    hi = x.astype(BF16)
    return hi, (x - hi.astype(F32)).astype(BF16)


def pair(x):
    return jnp.concatenate(halves(x), axis=1)


def twice(x, axis):
    return jnp.concatenate([x, x], axis=axis)


def stacked(x):
    hi, lo = halves(x)
    return jnp.concatenate([hi, hi, lo, lo], axis=0)


def dot(a, b):
    return jnp.dot(a, b, preferred_element_type=F32)


def dot_rows(a, b):
    return lax.dot_general(a, b, (((0,), (0,)), ((), ())), preferred_element_type=F32)


def fold(x):
    w = x.shape[1] // 2
    return x[:, :w] + x[:, w:]


def quad(x):
    h = x.shape[0] // 2
    y = fold(x)
    return y[:h] + y[h:]


def softplus_and_slope(x):
    e = jnp.exp(-jnp.abs(x))
    soft = jnp.maximum(x, 0.0) + jnp.log1p(e)
    slope = jnp.where(x >= 0.0, 1.0, e) / (1.0 + e)
    return soft, slope


MESH = pl.DeviceIdType.MESH


class Messages:
    def __init__(self, send_sems, recv_sems):
        self.send_sems, self.recv_sems, self.all = send_sems, recv_sems, {}

    def make(self, name, ref, peer):
        at = len(self.all)
        self.all[name] = pltpu.make_async_remote_copy(
            src_ref=ref, dst_ref=ref, send_sem=self.send_sems.at[at], recv_sem=self.recv_sems.at[at],
            device_id={"seq": peer}, device_id_type=MESH,
        )

    def start(self, *names):
        for name in names:
            self.all[name].start()

    def arrived(self, *names):
        for name in names:
            self.all[name].wait_recv()

    def sent(self):
        for copy in self.all.values():
            copy.wait_send()


def kernel(q_ref, k_ref, v_ref, qmap_ref, kmap_ref, gq_ref, gk_ref,
           q4, k4t, v4, k2t, sgk, state, norm, acc, top, tot, num, den, feat, a4, sgq, b4, b4t, v4t, adjs, adjt2, adjns, gkds,
           kbuf, vbuf, qbuf, grad, parts, mine, whole, squares, head_squares, seq_squares,
           kv_send, kv_recv, q_send, q_recv, rs_send, rs_recv, ag_send, ag_recv, sq_send, sq_recv):
    heads, dh = qmap_ref.shape[0], qmap_ref.shape[1]
    tok = q_ref.shape[0]
    me = lax.axis_index("seq")
    my_head = lax.axis_index("head")
    n_seq, n_head = kbuf.shape[0], head_squares.shape[0] + 1
    side = math.isqrt(n_seq)
    my_x, my_z = me // side, lax.rem(me, side)
    given = qbuf.shape[1] // dh
    kept = heads - given
    far = n_seq - 1 - me
    early = me < n_seq // 2
    main = list(range(kept))
    rest = list(range(kept, heads))
    guest = list(range(heads, heads + given))

    def at(dx, dz):
        return lax.rem(my_x + dx + side, side) * side + lax.rem(my_z + dz + side, side)

    barrier = pltpu.get_barrier_semaphore()
    for peer in (at(1, 0), at(-1, 0), at(0, 1), at(0, -1), far):
        pl.semaphore_signal(barrier, inc=1, device_id={"seq": peer}, device_id_type=MESH)

    def greet_head(k, _):
        pl.semaphore_signal(barrier, inc=1, device_id={"head": lax.rem(my_head + k, n_head)}, device_id_type=MESH)
        return 0

    lax.fori_loop(1, n_head, greet_head, 0)
    kbuf[me] = k_ref[...]
    vbuf[me] = v_ref[...]

    half = tok // 2
    msgs = Messages(kv_send, kv_recv)
    for tag, buf, flip in (("k", kbuf, False), ("v", vbuf, True)):
        def place(a, b):
            return at(b, a) if flip else at(a, b)

        def route(name, a, b, first):
            up = place(1, 0) if first else place(0, 1)
            down = place(-1, 0) if first else place(0, -1)
            msgs.make(tag + name + "+", buf.at[place(a, b)], up)
            msgs.make(tag + name + "-", buf.at[place(a, b)], down)
            pa, pb, na, nb = (a - 1, b, a + 1, b) if first else (a, b - 1, a, b + 1)
            msgs.make(tag + name + "++", buf.at[place(pa, pb), pl.ds(0, half)], up)
            msgs.make(tag + name + "--", buf.at[place(na, nb), pl.ds(half, half)], down)

        route("1", 0, 0, True)
        for name, a in (("a", 0), ("b", -1), ("c", 1), ("d", 2)):
            route(name, a, 0, False)

    def both(*names):
        return [t + x for t in "kv" for x in names]

    query_copy = pltpu.make_async_remote_copy(
        src_ref=q_ref.at[:, pl.ds(kept * dh, given * dh)], dst_ref=qbuf,
        send_sem=q_send.at[0], recv_sem=q_recv.at[0], device_id={"seq": far}, device_id_type=MESH,
    )

    scale = dh ** -0.5 * math.log2(math.e)
    rows = lax.broadcasted_iota(jnp.int32, (tok, tok), 0)
    cols = lax.broadcasted_iota(jnp.int32, (tok, tok), 1)
    causal = rows >= cols
    kmap2 = twice(pair(kmap_ref[0]), 0)

    def prepare(j):
        k, v = kbuf[j], vbuf[j]
        kt = k.T
        keys = stacked(kt * scale)
        k4t[j] = keys
        k2t[j] = jnp.concatenate(halves(kt), axis=0)
        v2 = pair(v)
        values = twice(v2, 0)
        v4[j] = values
        b, slope = softplus_and_slope(fold(dot(pair(k), kmap2)))
        sgk[j] = slope
        return keys, values, b, v2

    def diagonal(n, b, v):
        b4[n] = twice(pair(b), 0)
        b4t[n] = stacked(b.T)
        v4t[n] = stacked(v.T)

    def attend(group, keys, values, masked=False, fresh=False):
        scores = [dot(q4[h], keys) for h in group]
        if not fresh:
            before = [(top[h], tot[h], acc[h]) for h in group]
        found = []
        for i, s in enumerate(scores):
            if masked:
                s = jnp.where(causal, s, NEGATIVE)
            new = jnp.max(s, axis=1, keepdims=True)
            if fresh:
                new = jnp.broadcast_to(new, (tok, dh))
            else:
                new = jnp.maximum(before[i][0], new)
                alpha = jnp.exp2(before[i][0] - new)
            p = jnp.exp2(s - twice(new, 1))
            o = fold(dot(pair(p), values))
            t = fold(p)
            if not fresh:
                t = before[i][1] * alpha + t
                o = before[i][2] * alpha + o
            found.append((new, t, o))
        for h, (new, t, o) in zip(group, found):
            top[h], tot[h], acc[h] = new, t, o

    def load_queries(slots, source):
        for h, q in zip(slots, source):
            q4[h] = twice(pair(q), 1)

    def before(slots, names, n, j, fresh):
        values = v4[j]
        acts = [fold(dot(q4[h, :, : 2 * dh], twice(pair(qmap_ref[m]), 0))) for h, m in zip(slots, names)]
        soft = [softplus_and_slope(act) for act in acts]
        a4s = [twice(pair(a), 1) for a, _ in soft]
        for h, (a, slope), four in zip(slots, soft, a4s):
            feat[h], sgq[h], a4[h] = a, slope, four
        kers = [jnp.where(causal, dot(four, b4t[n]), 0.0) for four in a4s]
        nums = [fold(dot(pair(ker), values)) for ker in kers]
        for h, ker, nm in zip(slots, kers, nums):
            den[h] = jnp.broadcast_to(jnp.sum(ker, axis=1, keepdims=True), (tok, dh))
            num[h] = nm
        attend(slots, k4t[j], values, masked=True, fresh=fresh)

    def own_queries(slots):
        return [q_ref[:, h * dh : (h + 1) * dh] for h in slots]

    state[...] = jnp.zeros_like(state)
    norm[...] = jnp.zeros_like(norm)
    adjns[...] = jnp.zeros_like(adjns)
    adjt2[...] = jnp.zeros_like(adjt2)
    _, _, b_own, v2_own = prepare(me)
    diagonal(0, b_own, v_ref[...])
    state_own = quad(dot_rows(pair(b_own), v2_own))
    norm_own = jnp.sum(b_own, axis=0, keepdims=True)

    def add_state(n, s, b):
        state[n] += s
        norm[n] += b

    def begin(slots):
        load_queries(slots, own_queries(slots))
        before(slots, slots, 0, me, True)

    cut = kept // 2
    begin(main[:cut])
    pl.semaphore_wait(barrier, n_head + 4)
    msgs.start(*both("1+", "1-"))
    begin(main[cut:])
    msgs.start(*both("a+", "a-"))

    @pl.when(jnp.logical_not(early))
    def _():
        query_copy.start()

    @pl.when(early)
    def _():
        begin(rest)
        add_state(1, state_own, norm_own)

    msgs.arrived(*both("1+", "1-"))
    msgs.start(*both("1++", "1--", "b+", "b-", "c+", "c-"))
    msgs.arrived(*both("a+", "a-"))
    msgs.start(*both("a++", "a--"))

    @pl.when(early)
    def _():
        query_copy.wait_recv()
        load_queries(guest, [qbuf[:, i * dh : (i + 1) * dh] for i in range(given)])
        for h in guest:
            top[h] = jnp.full((tok, dh), NEGATIVE, F32)
            tot[h] = jnp.zeros((tok, dh), F32)
            acc[h] = jnp.zeros((tok, dh), F32)
        attend(guest, k4t[me], v4[me])

    def block(j):
        @pl.when(j < me)
        def _():
            keys, values, b, v2 = prepare(j)
            attend(main, keys, values)
            s, c = quad(dot_rows(pair(b), v2)), jnp.sum(b, axis=0, keepdims=True)
            add_state(0, s, c)
            add_state(1, s, c)

            @pl.when(early)
            def _():
                attend(rest + guest, keys, values)

        @pl.when(jnp.logical_and(j > me, j <= far))
        def _():
            keys, values, b, v2 = prepare(j)

            @pl.when(j < far)
            def _():
                attend(guest, keys, values)
                add_state(1, quad(dot_rows(pair(b), v2)), jnp.sum(b, axis=0, keepdims=True))

            @pl.when(j == far)
            def _():
                diagonal(1, b, vbuf[j])
                before(guest, rest, 1, j, False)

    order = (
        (0, 3), (0, 1), (3, 0), (1, 0), (0, 2), (2, 0), (3, 3), (3, 1), (1, 3), (1, 1),
        (3, 2), (1, 2), (2, 3), (2, 1), (2, 2),
    )

    def step(t, _):
        @pl.when(t == 4)
        def _():
            msgs.arrived(*both("1++", "1--"))
            msgs.start(*both("d+", "d-"))
            msgs.arrived(*both("a++", "a--"))

        @pl.when(t == 6)
        def _():
            msgs.arrived(*both("b+", "b-", "c+", "c-"))
            msgs.start(*both("b++", "b--", "c++", "c--"))

        @pl.when(t == 8)
        def _():
            msgs.arrived(*both("d+", "d-"))
            msgs.start(*both("d++", "d--"))

        @pl.when(t == 10)
        def _():
            msgs.arrived(*both("b++", "b--", "c++", "c--"))

        @pl.when(t == 14)
        def _():
            msgs.arrived(*both("d++", "d--"))

        dx, dz = jnp.int32(0), jnp.int32(0)
        for i, (ox, oz) in enumerate(order):
            dx = jnp.where(t == i, ox, dx)
            dz = jnp.where(t == i, oz, dz)
        block(at(dx, dz))
        return 0

    lax.fori_loop(0, n_seq - 1, step, 0)

    def after(slots, n):
        state2 = twice(pair(state[n]), 0)
        state2t = twice(pair(state[n].T), 0)
        norm_row = norm[n]
        feats = [feat[h] for h in slots]
        a2s = [a4[h, :, : 2 * dh] for h in slots]
        inter = [fold(dot(a2, state2)) for a2 in a2s]
        gns, gds = [], []
        for h, a, more in zip(slots, feats, inter):
            rden = 1.0 / (den[h] + jnp.sum(a * norm_row, axis=1, keepdims=True))
            student = (num[h] + more) * rden
            teacher = acc[h] / jnp.sum(tot[h], axis=1, keepdims=True)
            gn = (student - teacher) * rden
            gns.append(pair(gn))
            gds.append(-jnp.sum(gn * student, axis=1, keepdims=True))
        coups = [dot(twice(gn2, 1), v4t[n]) for gn2 in gns]
        c2s = [pair(jnp.where(causal, c + gd, 0.0)) for c, gd in zip(coups, gds)]
        gqs = [
            fold(dot(c2, b4[n])) + fold(dot(gn2, state2t)) + gd * norm_row
            for c2, gn2, gd in zip(c2s, gns, gds)
        ]
        grads = [quad(dot_rows(q4[h, :, : 2 * dh], pair(g * sgq[h]))) for h, g in zip(slots, gqs)]
        adj = sum(quad(dot_rows(a2, gn2)) for a2, gn2 in zip(a2s, gns))
        adjn = sum(jnp.sum(a * gd, axis=0, keepdims=True) for a, gd in zip(feats, gds))
        gkd = sum(quad(dot_rows(c2, a2)) for c2, a2 in zip(c2s, a2s))
        return grads, adj, adjn, gkd

    width = dh // n_seq
    groups = ((0, cut), (cut, heads - cut), (heads, 1))

    def rows_of(d):
        return pl.ds(pl.multiple_of(d * width, width), width)

    def scatter(g):
        first, count = groups[g]

        def send(k, _):
            peer = lax.rem(me + k, n_seq)
            pltpu.make_async_remote_copy(
                src_ref=grad.at[pl.ds(first, count), rows_of(peer)],
                dst_ref=parts.at[k - 1, pl.ds(first, count)],
                send_sem=rs_send.at[g], recv_sem=rs_recv.at[g],
                device_id={"seq": peer}, device_id_type=MESH,
            ).start()
            return 0

        lax.fori_loop(1, n_seq, send, 0)

    def all_of(ref, sem):
        pltpu.make_async_copy(ref, ref, sem).wait()

    def reduce(g):
        first, count = groups[g]
        span = pl.ds(first, count)
        all_of(parts.at[:, span], rs_recv.at[g])
        total = grad[span, rows_of(me)]
        for k in range(n_seq - 1):
            total = total + parts[k, span]
        mine[span] = total
        return jnp.sum(total * total, axis=0)

    def spread(g, first, count):
        span = pl.ds(first, count)
        whole[span, rows_of(me)] = mine[span]

        def send(k, _):
            pltpu.make_async_remote_copy(
                src_ref=mine.at[span],
                dst_ref=whole.at[span, rows_of(me)],
                send_sem=ag_send.at[g], recv_sem=ag_recv.at[g],
                device_id={"seq": lax.rem(me + k, n_seq)}, device_id_type=MESH,
            ).start()
            return 0

        lax.fori_loop(1, n_seq, send, 0)

    def keep(grads, slots):
        for h, g in zip(slots, grads):
            grad[h] = g

    grads, adj, adjn, gkd = after(main[:cut], 0)
    keep(grads, main[:cut])
    scatter(0)
    grads, adj_b, adjn_b, gkd_b = after(main[cut:], 0)
    keep(grads, main[cut:])
    adjs[...] = adj + adj_b
    adjns[0] = adjn + adjn_b
    gkds[0] = gkd + gkd_b

    @pl.when(early)
    def _():
        grads, adj, adjn, gkd = after(rest, 0)
        guests, adj_g, adjn_g, gkd_g = after(guest, 1)
        keep([u + w for u, w in zip(grads, guests)], rest)
        adjs[...] += adj + adj_g
        adjns[0] += adjn + adjn_g
        gkds[0] += gkd
        gkds[1] = gkd_g
        adjt2[1] = twice(pair(adj_g.T), 0)
        adjns[1] = adjn_g

    @pl.when(jnp.logical_not(early))
    def _():
        for h in rest:
            grad[h] = jnp.zeros((dh, dh), F32)

    scatter(1)

    adjt2[0] = twice(pair(adjs[...].T), 0)
    limit = jnp.where(early, far, me)

    def diagonal_grad(n, j):
        return quad(dot(k2t[j], pair(gkds[n] * sgk[j])))

    grad[heads] = diagonal_grad(0, me)

    @pl.when(early)
    def _():
        grad[heads] += diagonal_grad(1, far)

    batch = 4

    def later(c, _):
        js = [batch * c + i for i in range(batch)]
        inside = [j < limit for j in js]
        js = [jnp.where(ok, j, me) for ok, j in zip(inside, js)]
        which = [jnp.where(j < me, 0, 1) for j in js]
        outs = [fold(dot(v4[j, :tok], adjt2[w])) + adjns[w] for j, w in zip(js, which)]
        dks = [pair(jnp.where(ok, g * sgk[j], 0.0)) for ok, j, g in zip(inside, js, outs)]
        grad[heads] += quad(sum(dot(k2t[j], dk) for j, dk in zip(js, dks)))
        return 0

    lax.fori_loop(0, (limit + batch - 1) // batch, later, 0)
    scatter(2)
    early_squares = reduce(0) + reduce(1)
    spread(0, 0, heads)
    squares[0] = early_squares + reduce(2)

    def send_head(k, _):
        pltpu.make_async_remote_copy(
            src_ref=squares.at[0], dst_ref=head_squares.at[k - 1],
            send_sem=sq_send.at[0], recv_sem=sq_recv.at[0],
            device_id={"head": lax.rem(my_head + k, n_head)}, device_id_type=MESH,
        ).start()
        return 0

    def send_seq(k, _):
        pltpu.make_async_remote_copy(
            src_ref=squares.at[1], dst_ref=seq_squares.at[k - 1],
            send_sem=sq_send.at[1], recv_sem=sq_recv.at[1],
            device_id={"seq": lax.rem(me + k, n_seq)}, device_id_type=MESH,
        ).start()
        return 0

    lax.fori_loop(1, n_head, send_head, 0)
    spread(1, heads, 1)
    all_of(head_squares, sq_recv.at[0])
    squares[1] = squares[0] + jnp.sum(head_squares[...], axis=0)
    lax.fori_loop(1, n_seq, send_seq, 0)
    all_of(seq_squares, sq_recv.at[1])
    square = jnp.sum(squares[1] + jnp.sum(seq_squares[...], axis=0))
    size = (heads + 1) * n_head * dh * grad.shape[2]
    factor = 1.0 / jnp.sqrt(jnp.broadcast_to(square / size + EPSILON, (1, dh)))
    arrived = (parts.at[:, pl.ds(0, heads)], parts.at[:, pl.ds(heads, 1)])
    for g in range(2):
        all_of(arrived[g], ag_recv.at[g])
    gq_ref[...] = whole[pl.ds(0, heads)] * factor
    gk_ref[...] = whole[pl.ds(heads, 1)] * factor

    msgs.sent()

    @pl.when(jnp.logical_not(early))
    def _():
        query_copy.wait_send()

    for g in range(3):
        first, count = groups[g]
        all_of(parts.at[:, pl.ds(first, count)], rs_send.at[g])
    for g in range(2):
        all_of(arrived[g], ag_send.at[g])
    all_of(head_squares, sq_send.at[0])
    all_of(seq_squares, sq_send.at[1])


def on_device(queries, key_heads, value_heads, query_map, key_map):
    tok = queries.shape[0]
    heads, dh, feats = query_map.shape
    n = lax.axis_size("seq")
    given = heads // 8
    slots = heads + given
    return pl.pallas_call(
        kernel,
        out_shape=(jax.ShapeDtypeStruct((heads, dh, feats), F32), jax.ShapeDtypeStruct((1, dh, feats), F32)),
        in_specs=[pl.BlockSpec(memory_space=pltpu.VMEM)] * 5,
        out_specs=(pl.BlockSpec(memory_space=pltpu.VMEM),) * 2,
        scratch_shapes=[
            pltpu.VMEM((slots, tok, 4 * dh), BF16),
            pltpu.VMEM((n, 4 * dh, tok), BF16),
            pltpu.VMEM((n, 2 * tok, 2 * dh), BF16),
            pltpu.VMEM((n, 2 * dh, tok), BF16),
            pltpu.VMEM((n, tok, feats), F32),
            pltpu.VMEM((2, feats, dh), F32),
            pltpu.VMEM((2, 1, feats), F32),
        ] + [pltpu.VMEM((slots, tok, dh), F32)] * 6 + [
            pltpu.VMEM((slots, tok, 4 * feats), BF16),
            pltpu.VMEM((slots, tok, feats), F32),
            pltpu.VMEM((2, 2 * tok, 2 * feats), BF16),
            pltpu.VMEM((2, 4 * feats, tok), BF16),
            pltpu.VMEM((2, 4 * dh, tok), BF16),
            pltpu.VMEM((feats, dh), F32),
            pltpu.VMEM((2, 2 * dh, 2 * feats), BF16),
            pltpu.VMEM((2, 1, feats), F32),
            pltpu.VMEM((2, tok, feats), F32),
            pltpu.VMEM((n, tok, dh), F32),
            pltpu.VMEM((n, tok, dh), F32),
            pltpu.VMEM((tok, given * dh), F32),
            pltpu.VMEM((heads + 1, dh, feats), F32),
            pltpu.VMEM((n - 1, heads + 1, dh // n, feats), F32),
            pltpu.VMEM((heads + 1, dh // n, feats), F32),
            pltpu.VMEM((heads + 1, dh, feats), F32),
            pltpu.VMEM((2, dh // n, feats), F32),
            pltpu.VMEM((lax.axis_size("head") - 1, dh // n, feats), F32),
            pltpu.VMEM((n - 1, dh // n, feats), F32),
            pltpu.SemaphoreType.DMA((40,)),
            pltpu.SemaphoreType.DMA((40,)),
            pltpu.SemaphoreType.DMA((1,)),
            pltpu.SemaphoreType.DMA((1,)),
        ] + [pltpu.SemaphoreType.DMA((3,))] * 2 + [pltpu.SemaphoreType.DMA((2,))] * 4,
        compiler_params=pltpu.CompilerParams(vmem_limit_bytes=56 * 2**20, collective_id=0, has_side_effects=True),
    )(queries, key_heads, value_heads, query_map, key_map)


def solution(mesh):
    return jax.shard_map(
        on_device,
        mesh=mesh,
        in_specs=(P("seq", "head"), P("seq", "head"), P("seq", "head"), P("head"), P("head")),
        out_specs=(P("head"), P("head")),
        check_vma=False,
    )
```

```python
import math

import jax
import jax.numpy as jnp
from jax import lax
from jax.experimental import pallas as pl
from jax.experimental.pallas import tpu as pltpu
from jax.sharding import PartitionSpec as P

NEGATIVE = -1e30
EPSILON = 1e-06
F32 = jnp.float32
BF16 = jnp.bfloat16


def halves(x):
    hi = x.astype(BF16)
    return hi, (x - hi.astype(F32)).astype(BF16)


def pair(x):
    return jnp.concatenate(halves(x), axis=1)


def twice(x, axis):
    return jnp.concatenate([x, x], axis=axis)


def stacked(x):
    hi, lo = halves(x)
    return jnp.concatenate([hi, hi, lo, lo], axis=0)


def dot(a, b):
    return jnp.dot(a, b, preferred_element_type=F32)


def dot_rows(a, b):
    return lax.dot_general(a, b, (((0,), (0,)), ((), ())), preferred_element_type=F32)


def fold(x):
    w = x.shape[1] // 2
    return x[:, :w] + x[:, w:]


def quad(x):
    h = x.shape[0] // 2
    y = fold(x)
    return y[:h] + y[h:]


def softplus_and_slope(x):
    e = jnp.exp(-jnp.abs(x))
    soft = jnp.maximum(x, 0.0) + jnp.log1p(e)
    slope = jnp.where(x >= 0.0, 1.0, e) / (1.0 + e)
    return soft, slope


MESH = pl.DeviceIdType.MESH


class Messages:
    def __init__(self, send_sems, recv_sems):
        self.send_sems, self.recv_sems, self.all = send_sems, recv_sems, {}

    def make(self, name, ref, peer):
        at = len(self.all)
        self.all[name] = pltpu.make_async_remote_copy(
            src_ref=ref, dst_ref=ref, send_sem=self.send_sems.at[at], recv_sem=self.recv_sems.at[at],
            device_id={"seq": peer}, device_id_type=MESH,
        )

    def start(self, *names):
        for name in names:
            self.all[name].start()

    def arrived(self, *names):
        for name in names:
            self.all[name].wait_recv()

    def sent(self):
        for copy in self.all.values():
            copy.wait_send()


def kernel(q_ref, k_ref, v_ref, qmap_ref, kmap_ref, gq_ref, gk_ref,
           q4, k4t, v4, k2t, sgk, state, norm, acc, top, tot, num, den, feat, a4, sgq, b4, b4t, v4t, adjs, adjt2, adjns, gkds,
           kbuf, vbuf, qbuf, grad, parts, mine, whole, squares, head_squares, seq_squares,
           kv_send, kv_recv, q_send, q_recv, rs_send, rs_recv, ag_send, ag_recv, sq_send, sq_recv):
    heads, dh = qmap_ref.shape[0], qmap_ref.shape[1]
    tok = q_ref.shape[0]
    me = lax.axis_index("seq")
    my_head = lax.axis_index("head")
    n_seq, n_head = kbuf.shape[0], head_squares.shape[0] + 1
    side = math.isqrt(n_seq)
    my_x, my_z = me // side, lax.rem(me, side)
    given = qbuf.shape[1] // dh
    kept = heads - given
    far = n_seq - 1 - me
    early = me < n_seq // 2
    main = list(range(kept))
    rest = list(range(kept, heads))
    guest = list(range(heads, heads + given))

    def at(dx, dz):
        return lax.rem(my_x + dx + side, side) * side + lax.rem(my_z + dz + side, side)

    barrier = pltpu.get_barrier_semaphore()
    for peer in (at(1, 0), at(-1, 0), at(0, 1), at(0, -1), far):
        pl.semaphore_signal(barrier, inc=1, device_id={"seq": peer}, device_id_type=MESH)

    def greet_head(k, _):
        pl.semaphore_signal(barrier, inc=1, device_id={"head": lax.rem(my_head + k, n_head)}, device_id_type=MESH)
        return 0

    lax.fori_loop(1, n_head, greet_head, 0)
    kbuf[me] = k_ref[...]
    vbuf[me] = v_ref[...]

    half = tok // 2
    msgs = Messages(kv_send, kv_recv)
    for tag, buf, flip in (("k", kbuf, False), ("v", vbuf, True)):
        def place(a, b):
            return at(b, a) if flip else at(a, b)

        def route(name, a, b, first):
            up = place(1, 0) if first else place(0, 1)
            down = place(-1, 0) if first else place(0, -1)
            msgs.make(tag + name + "+", buf.at[place(a, b)], up)
            msgs.make(tag + name + "-", buf.at[place(a, b)], down)
            pa, pb, na, nb = (a - 1, b, a + 1, b) if first else (a, b - 1, a, b + 1)
            msgs.make(tag + name + "++", buf.at[place(pa, pb), pl.ds(0, half)], up)
            msgs.make(tag + name + "--", buf.at[place(na, nb), pl.ds(half, half)], down)

        route("1", 0, 0, True)
        for name, a in (("a", 0), ("b", -1), ("c", 1), ("d", 2)):
            route(name, a, 0, False)

    def both(*names):
        return [t + x for t in "kv" for x in names]

    query_copy = pltpu.make_async_remote_copy(
        src_ref=q_ref.at[:, pl.ds(kept * dh, given * dh)], dst_ref=qbuf,
        send_sem=q_send.at[0], recv_sem=q_recv.at[0], device_id={"seq": far}, device_id_type=MESH,
    )

    scale = dh ** -0.5 * math.log2(math.e)
    rows = lax.broadcasted_iota(jnp.int32, (tok, tok), 0)
    cols = lax.broadcasted_iota(jnp.int32, (tok, tok), 1)
    causal = rows >= cols
    kmap2 = twice(pair(kmap_ref[0]), 0)

    def prepare(j):
        k, v = kbuf[j], vbuf[j]
        kt = k.T
        keys = stacked(kt * scale)
        k4t[j] = keys
        k2t[j] = jnp.concatenate(halves(kt), axis=0)
        v2 = pair(v)
        values = twice(v2, 0)
        v4[j] = values
        b, slope = softplus_and_slope(fold(dot(pair(k), kmap2)))
        sgk[j] = slope
        return keys, values, b, v2

    def diagonal(n, b, v):
        b4[n] = twice(pair(b), 0)
        b4t[n] = stacked(b.T)
        v4t[n] = stacked(v.T)

    def attend(group, keys, values, masked=False, fresh=False):
        scores = [dot(q4[h, :, : 3 * dh], keys[: 3 * dh]) for h in group]
        if not fresh:
            before = [(top[h], tot[h], acc[h]) for h in group]
        found = []
        for i, s in enumerate(scores):
            if masked:
                s = jnp.where(causal, s, NEGATIVE)
            new = jnp.max(s, axis=1, keepdims=True)
            if fresh:
                new = jnp.broadcast_to(new, (tok, dh))
            else:
                new = jnp.maximum(before[i][0], new)
                alpha = jnp.exp2(before[i][0] - new)
            p = jnp.exp2(s - twice(new, 1))
            hi, lo = halves(p)
            o = fold(dot(hi, values[:tok]) + dot(lo, values[:tok]))
            t = fold(p)
            if not fresh:
                t = before[i][1] * alpha + t
                o = before[i][2] * alpha + o
            found.append((new, t, o))
        for h, (new, t, o) in zip(group, found):
            top[h], tot[h], acc[h] = new, t, o

    def load_queries(slots, source):
        for h, q in zip(slots, source):
            q4[h] = twice(pair(q), 1)

    def before(slots, names, n, j, fresh):
        values = v4[j]
        acts = [fold(dot(q4[h, :, : 2 * dh], twice(pair(qmap_ref[m]), 0))) for h, m in zip(slots, names)]
        soft = [softplus_and_slope(act) for act in acts]
        a4s = [twice(pair(a), 1) for a, _ in soft]
        for h, (a, slope), four in zip(slots, soft, a4s):
            feat[h], sgq[h], a4[h] = a, slope, four
        kers = [jnp.where(causal, dot(four, b4t[n]), 0.0) for four in a4s]
        nums = [fold(dot(pair(ker), values)) for ker in kers]
        for h, ker, nm in zip(slots, kers, nums):
            den[h] = jnp.broadcast_to(jnp.sum(ker, axis=1, keepdims=True), (tok, dh))
            num[h] = nm
        attend(slots, k4t[j], values, masked=True, fresh=fresh)

    def own_queries(slots):
        return [q_ref[:, h * dh : (h + 1) * dh] for h in slots]

    state[...] = jnp.zeros_like(state)
    norm[...] = jnp.zeros_like(norm)
    adjns[...] = jnp.zeros_like(adjns)
    adjt2[...] = jnp.zeros_like(adjt2)
    _, _, b_own, v2_own = prepare(me)
    diagonal(0, b_own, v_ref[...])
    state_own = quad(dot_rows(pair(b_own), v2_own))
    norm_own = jnp.sum(b_own, axis=0, keepdims=True)

    def add_state(n, s, b):
        state[n] += s
        norm[n] += b

    def begin(slots):
        load_queries(slots, own_queries(slots))
        before(slots, slots, 0, me, True)

    cut = (kept + 1) // 2
    begin(main[:cut])
    pl.semaphore_wait(barrier, n_head + 4)
    msgs.start(*both("1+", "1-"))
    begin(main[cut:])
    msgs.start(*both("a+", "a-"))

    @pl.when(jnp.logical_not(early))
    def _():
        query_copy.start()

    @pl.when(early)
    def _():
        begin(rest)
        add_state(1, state_own, norm_own)

    msgs.arrived(*both("1+", "1-"))
    msgs.start(*both("1++", "1--", "b+", "b-", "c+", "c-"))
    msgs.arrived(*both("a+", "a-"))
    msgs.start(*both("a++", "a--"))

    @pl.when(early)
    def _():
        query_copy.wait_recv()
        load_queries(guest, [qbuf[:, i * dh : (i + 1) * dh] for i in range(given)])
        for h in guest:
            top[h] = jnp.full((tok, dh), NEGATIVE, F32)
            tot[h] = jnp.zeros((tok, dh), F32)
            acc[h] = jnp.zeros((tok, dh), F32)
        attend(guest, k4t[me], v4[me])

    def block(j):
        @pl.when(j < me)
        def _():
            keys, values, b, v2 = prepare(j)
            attend(main, keys, values)
            s, c = quad(dot_rows(pair(b), v2)), jnp.sum(b, axis=0, keepdims=True)
            add_state(0, s, c)
            add_state(1, s, c)

            @pl.when(early)
            def _():
                attend(rest + guest, keys, values)

        @pl.when(jnp.logical_and(j > me, j <= far))
        def _():
            keys, values, b, v2 = prepare(j)

            @pl.when(j < far)
            def _():
                attend(guest, keys, values)
                add_state(1, quad(dot_rows(pair(b), v2)), jnp.sum(b, axis=0, keepdims=True))

            @pl.when(j == far)
            def _():
                diagonal(1, b, vbuf[j])
                before(guest, rest, 1, j, False)

    order = (
        (0, 3), (0, 1), (3, 0), (1, 0), (0, 2), (2, 0), (3, 3), (3, 1), (1, 3), (1, 1),
        (3, 2), (1, 2), (2, 3), (2, 1), (2, 2),
    )

    def step(t, _):
        @pl.when(t == 4)
        def _():
            msgs.arrived(*both("1++", "1--"))
            msgs.start(*both("d+", "d-"))
            msgs.arrived(*both("a++", "a--"))

        @pl.when(t == 6)
        def _():
            msgs.arrived(*both("b+", "b-", "c+", "c-"))
            msgs.start(*both("b++", "b--", "c++", "c--"))

        @pl.when(t == 8)
        def _():
            msgs.arrived(*both("d+", "d-"))
            msgs.start(*both("d++", "d--"))

        @pl.when(t == 10)
        def _():
            msgs.arrived(*both("b++", "b--", "c++", "c--"))

        @pl.when(t == 14)
        def _():
            msgs.arrived(*both("d++", "d--"))

        dx, dz = jnp.int32(0), jnp.int32(0)
        for i, (ox, oz) in enumerate(order):
            dx = jnp.where(t == i, ox, dx)
            dz = jnp.where(t == i, oz, dz)
        block(at(dx, dz))
        return 0

    lax.fori_loop(0, n_seq - 1, step, 0)

    def after(slots, n):
        state2 = twice(pair(state[n]), 0)
        state2t = twice(pair(state[n].T), 0)
        norm_row = norm[n]
        feats = [feat[h] for h in slots]
        a2s = [a4[h, :, : 2 * dh] for h in slots]
        inter = [fold(dot(a2, state2)) for a2 in a2s]
        gns, gds = [], []
        for h, a, more in zip(slots, feats, inter):
            rden = 1.0 / (den[h] + jnp.sum(a * norm_row, axis=1, keepdims=True))
            student = (num[h] + more) * rden
            teacher = acc[h] / jnp.sum(tot[h], axis=1, keepdims=True)
            gn = (student - teacher) * rden
            gns.append(pair(gn))
            gds.append(-jnp.sum(gn * student, axis=1, keepdims=True))
        coups = [dot(twice(gn2, 1), v4t[n]) for gn2 in gns]
        c2s = [pair(jnp.where(causal, c + gd, 0.0)) for c, gd in zip(coups, gds)]
        gqs = [
            fold(dot(c2, b4[n])) + fold(dot(gn2, state2t)) + gd * norm_row
            for c2, gn2, gd in zip(c2s, gns, gds)
        ]
        grads = [quad(dot_rows(q4[h, :, : 2 * dh], pair(g * sgq[h]))) for h, g in zip(slots, gqs)]
        adj = sum(quad(dot_rows(a2, gn2)) for a2, gn2 in zip(a2s, gns))
        adjn = sum(jnp.sum(a * gd, axis=0, keepdims=True) for a, gd in zip(feats, gds))
        gkd = sum(quad(dot_rows(c2, a2)) for c2, a2 in zip(c2s, a2s))
        return grads, adj, adjn, gkd

    width = dh // n_seq
    groups = ((0, cut), (cut, heads - cut), (heads, 1))

    def rows_of(d):
        return pl.ds(pl.multiple_of(d * width, width), width)

    def scatter(g):
        first, count = groups[g]

        def send(k, _):
            peer = lax.rem(me + k, n_seq)
            pltpu.make_async_remote_copy(
                src_ref=grad.at[pl.ds(first, count), rows_of(peer)],
                dst_ref=parts.at[k - 1, pl.ds(first, count)],
                send_sem=rs_send.at[g], recv_sem=rs_recv.at[g],
                device_id={"seq": peer}, device_id_type=MESH,
            ).start()
            return 0

        lax.fori_loop(1, n_seq, send, 0)

    def all_of(ref, sem):
        pltpu.make_async_copy(ref, ref, sem).wait()

    def reduce(g):
        first, count = groups[g]
        span = pl.ds(first, count)
        all_of(parts.at[:, span], rs_recv.at[g])
        total = grad[span, rows_of(me)]
        for k in range(n_seq - 1):
            total = total + parts[k, span]
        mine[span] = total
        return jnp.sum(total * total, axis=0)

    def spread(g, first, count):
        span = pl.ds(first, count)
        whole[span, rows_of(me)] = mine[span]

        def send(k, _):
            pltpu.make_async_remote_copy(
                src_ref=mine.at[span],
                dst_ref=whole.at[span, rows_of(me)],
                send_sem=ag_send.at[g], recv_sem=ag_recv.at[g],
                device_id={"seq": lax.rem(me + k, n_seq)}, device_id_type=MESH,
            ).start()
            return 0

        lax.fori_loop(1, n_seq, send, 0)

    def keep(grads, slots):
        for h, g in zip(slots, grads):
            grad[h] = g

    grads, adj, adjn, gkd = after(main[:cut], 0)
    keep(grads, main[:cut])
    scatter(0)
    grads, adj_b, adjn_b, gkd_b = after(main[cut:], 0)
    keep(grads, main[cut:])
    adjs[...] = adj + adj_b
    adjns[0] = adjn + adjn_b
    gkds[0] = gkd + gkd_b

    @pl.when(early)
    def _():
        grads, adj, adjn, gkd = after(rest, 0)
        guests, adj_g, adjn_g, gkd_g = after(guest, 1)
        keep([u + w for u, w in zip(grads, guests)], rest)
        adjs[...] += adj + adj_g
        adjns[0] += adjn + adjn_g
        gkds[0] += gkd
        gkds[1] = gkd_g
        adjt2[1] = twice(pair(adj_g.T), 0)
        adjns[1] = adjn_g

    @pl.when(jnp.logical_not(early))
    def _():
        for h in rest:
            grad[h] = jnp.zeros((dh, dh), F32)

    scatter(1)

    adjt2[0] = twice(pair(adjs[...].T), 0)
    limit = jnp.where(early, far, me)

    def diagonal_grad(n, j):
        return quad(dot(k2t[j], pair(gkds[n] * sgk[j])))

    grad[heads] = diagonal_grad(0, me)

    @pl.when(early)
    def _():
        grad[heads] += diagonal_grad(1, far)

    batch = 8

    def later(c, _):
        js = [batch * c + i for i in range(batch)]
        inside = [j < limit for j in js]
        js = [jnp.where(ok, j, me) for ok, j in zip(inside, js)]
        which = [jnp.where(j < me, 0, 1) for j in js]
        outs = [fold(dot(v4[j, :tok], adjt2[w])) + adjns[w] for j, w in zip(js, which)]
        dks = [pair(jnp.where(ok, g * sgk[j], 0.0)) for ok, j, g in zip(inside, js, outs)]
        grad[heads] += quad(sum(dot(k2t[j], dk) for j, dk in zip(js, dks)))
        return 0

    lax.fori_loop(0, (limit + batch - 1) // batch, later, 0)
    scatter(2)
    early_squares = reduce(0) + reduce(1)
    spread(0, 0, heads)
    squares[0] = early_squares + reduce(2)

    def send_head(k, _):
        pltpu.make_async_remote_copy(
            src_ref=squares.at[0], dst_ref=head_squares.at[k - 1],
            send_sem=sq_send.at[0], recv_sem=sq_recv.at[0],
            device_id={"head": lax.rem(my_head + k, n_head)}, device_id_type=MESH,
        ).start()
        return 0

    def send_seq(k, _):
        pltpu.make_async_remote_copy(
            src_ref=squares.at[1], dst_ref=seq_squares.at[k - 1],
            send_sem=sq_send.at[1], recv_sem=sq_recv.at[1],
            device_id={"seq": lax.rem(me + k, n_seq)}, device_id_type=MESH,
        ).start()
        return 0

    lax.fori_loop(1, n_head, send_head, 0)
    spread(1, heads, 1)
    all_of(head_squares, sq_recv.at[0])
    squares[1] = squares[0] + jnp.sum(head_squares[...], axis=0)
    lax.fori_loop(1, n_seq, send_seq, 0)
    all_of(seq_squares, sq_recv.at[1])
    square = jnp.sum(squares[1] + jnp.sum(seq_squares[...], axis=0))
    size = (heads + 1) * n_head * dh * grad.shape[2]
    factor = 1.0 / jnp.sqrt(jnp.broadcast_to(square / size + EPSILON, (1, dh)))
    arrived = (parts.at[:, pl.ds(0, heads)], parts.at[:, pl.ds(heads, 1)])
    for g in range(2):
        all_of(arrived[g], ag_recv.at[g])
    gq_ref[...] = whole[pl.ds(0, heads)] * factor
    gk_ref[...] = whole[pl.ds(heads, 1)] * factor

    msgs.sent()

    @pl.when(jnp.logical_not(early))
    def _():
        query_copy.wait_send()

    for g in range(3):
        first, count = groups[g]
        all_of(parts.at[:, pl.ds(first, count)], rs_send.at[g])
    for g in range(2):
        all_of(arrived[g], ag_send.at[g])
    all_of(head_squares, sq_send.at[0])
    all_of(seq_squares, sq_send.at[1])


def on_device(queries, key_heads, value_heads, query_map, key_map):
    tok = queries.shape[0]
    heads, dh, feats = query_map.shape
    n = lax.axis_size("seq")
    given = heads // 8
    slots = heads + given
    return pl.pallas_call(
        kernel,
        out_shape=(jax.ShapeDtypeStruct((heads, dh, feats), F32), jax.ShapeDtypeStruct((1, dh, feats), F32)),
        in_specs=[pl.BlockSpec(memory_space=pltpu.VMEM)] * 5,
        out_specs=(pl.BlockSpec(memory_space=pltpu.VMEM),) * 2,
        scratch_shapes=[
            pltpu.VMEM((slots, tok, 4 * dh), BF16),
            pltpu.VMEM((n, 4 * dh, tok), BF16),
            pltpu.VMEM((n, 2 * tok, 2 * dh), BF16),
            pltpu.VMEM((n, 2 * dh, tok), BF16),
            pltpu.VMEM((n, tok, feats), F32),
            pltpu.VMEM((2, feats, dh), F32),
            pltpu.VMEM((2, 1, feats), F32),
        ] + [pltpu.VMEM((slots, tok, dh), F32)] * 6 + [
            pltpu.VMEM((slots, tok, 4 * feats), BF16),
            pltpu.VMEM((slots, tok, feats), F32),
            pltpu.VMEM((2, 2 * tok, 2 * feats), BF16),
            pltpu.VMEM((2, 4 * feats, tok), BF16),
            pltpu.VMEM((2, 4 * dh, tok), BF16),
            pltpu.VMEM((feats, dh), F32),
            pltpu.VMEM((2, 2 * dh, 2 * feats), BF16),
            pltpu.VMEM((2, 1, feats), F32),
            pltpu.VMEM((2, tok, feats), F32),
            pltpu.VMEM((n, tok, dh), F32),
            pltpu.VMEM((n, tok, dh), F32),
            pltpu.VMEM((tok, given * dh), F32),
            pltpu.VMEM((heads + 1, dh, feats), F32),
            pltpu.VMEM((n - 1, heads + 1, dh // n, feats), F32),
            pltpu.VMEM((heads + 1, dh // n, feats), F32),
            pltpu.VMEM((heads + 1, dh, feats), F32),
            pltpu.VMEM((2, dh // n, feats), F32),
            pltpu.VMEM((lax.axis_size("head") - 1, dh // n, feats), F32),
            pltpu.VMEM((n - 1, dh // n, feats), F32),
            pltpu.SemaphoreType.DMA((40,)),
            pltpu.SemaphoreType.DMA((40,)),
            pltpu.SemaphoreType.DMA((1,)),
            pltpu.SemaphoreType.DMA((1,)),
        ] + [pltpu.SemaphoreType.DMA((3,))] * 2 + [pltpu.SemaphoreType.DMA((2,))] * 4,
        compiler_params=pltpu.CompilerParams(vmem_limit_bytes=56 * 2**20, collective_id=0, has_side_effects=True),
    )(queries, key_heads, value_heads, query_map, key_map)


def solution(mesh):
    return jax.shard_map(
        on_device,
        mesh=mesh,
        in_specs=(P("seq", "head"), P("seq", "head"), P("seq", "head"), P("head"), P("head")),
        out_specs=(P("head"), P("head")),
        check_vma=False,
    )
```

```python
import math

import jax
import jax.numpy as jnp
from jax import lax
from jax.experimental import pallas as pl
from jax.experimental.pallas import tpu as pltpu
from jax.sharding import PartitionSpec as P

NEGATIVE = -1e30
EPSILON = 1e-06
F32 = jnp.float32
BF16 = jnp.bfloat16


def halves(x):
    hi = x.astype(BF16)
    return hi, (x - hi.astype(F32)).astype(BF16)


def pair(x):
    return jnp.concatenate(halves(x), axis=1)


def twice(x, axis):
    return jnp.concatenate([x, x], axis=axis)


def stacked(x):
    hi, lo = halves(x)
    return jnp.concatenate([hi, hi, lo, lo], axis=0)


def dot(a, b):
    return jnp.dot(a, b, preferred_element_type=F32)


def dot_rows(a, b):
    return lax.dot_general(a, b, (((0,), (0,)), ((), ())), preferred_element_type=F32)


def fold(x):
    w = x.shape[1] // 2
    return x[:, :w] + x[:, w:]


def quad(x):
    h = x.shape[0] // 2
    y = fold(x)
    return y[:h] + y[h:]


def softplus_and_slope(x):
    e = jnp.exp(-jnp.abs(x))
    soft = jnp.maximum(x, 0.0) + jnp.log1p(e)
    slope = jnp.where(x >= 0.0, 1.0, e) / (1.0 + e)
    return soft, slope


MESH = pl.DeviceIdType.MESH


class Messages:
    def __init__(self, send_sems, recv_sems):
        self.send_sems, self.recv_sems, self.all = send_sems, recv_sems, {}

    def make(self, name, ref, peer):
        at = len(self.all)
        self.all[name] = pltpu.make_async_remote_copy(
            src_ref=ref, dst_ref=ref, send_sem=self.send_sems.at[at], recv_sem=self.recv_sems.at[at],
            device_id={"seq": peer}, device_id_type=MESH,
        )

    def start(self, *names):
        for name in names:
            self.all[name].start()

    def arrived(self, *names):
        for name in names:
            self.all[name].wait_recv()

    def sent(self):
        for copy in self.all.values():
            copy.wait_send()


def kernel(q_ref, k_ref, v_ref, qmap_ref, kmap_ref, gq_ref, gk_ref,
           q4, k4t, v4, k2t, sgk, state, norm, acc, top, tot, num, den, feat, a4, sgq, b4, b4t, v4t, adjs, adjt2, adjns, gkds,
           kbuf, vbuf, qbuf, grad, parts, mine, whole, squares, head_squares, seq_squares,
           kv_send, kv_recv, q_send, q_recv, rs_send, rs_recv, ag_send, ag_recv, sq_send, sq_recv):
    heads, dh = qmap_ref.shape[0], qmap_ref.shape[1]
    tok = q_ref.shape[0]
    me = lax.axis_index("seq")
    my_head = lax.axis_index("head")
    n_seq, n_head = kbuf.shape[0], head_squares.shape[0] + 1
    side = math.isqrt(n_seq)
    my_x, my_z = me // side, lax.rem(me, side)
    given = qbuf.shape[1] // dh
    kept = heads - given
    far = n_seq - 1 - me
    early = me < n_seq // 2
    main = list(range(kept))
    rest = list(range(kept, heads))
    guest = list(range(heads, heads + given))

    def at(dx, dz):
        return lax.rem(my_x + dx + side, side) * side + lax.rem(my_z + dz + side, side)

    barrier = pltpu.get_barrier_semaphore()
    for peer in (at(1, 0), at(-1, 0), at(0, 1), at(0, -1), far):
        pl.semaphore_signal(barrier, inc=1, device_id={"seq": peer}, device_id_type=MESH)

    def greet_head(k, _):
        pl.semaphore_signal(barrier, inc=1, device_id={"head": lax.rem(my_head + k, n_head)}, device_id_type=MESH)
        return 0

    lax.fori_loop(1, n_head, greet_head, 0)
    kbuf[me] = k_ref[...]
    vbuf[me] = v_ref[...]

    half = tok // 2
    msgs = Messages(kv_send, kv_recv)
    for tag, buf, flip in (("k", kbuf, False), ("v", vbuf, True)):
        def place(a, b):
            return at(b, a) if flip else at(a, b)

        def route(name, a, b, first):
            up = place(1, 0) if first else place(0, 1)
            down = place(-1, 0) if first else place(0, -1)
            msgs.make(tag + name + "+", buf.at[place(a, b)], up)
            msgs.make(tag + name + "-", buf.at[place(a, b)], down)
            pa, pb, na, nb = (a - 1, b, a + 1, b) if first else (a, b - 1, a, b + 1)
            msgs.make(tag + name + "++", buf.at[place(pa, pb), pl.ds(0, half)], up)
            msgs.make(tag + name + "--", buf.at[place(na, nb), pl.ds(half, half)], down)

        route("1", 0, 0, True)
        for name, a in (("a", 0), ("b", -1), ("c", 1), ("d", 2)):
            route(name, a, 0, False)

    def both(*names):
        return [t + x for t in "kv" for x in names]

    query_copy = pltpu.make_async_remote_copy(
        src_ref=q_ref.at[:, pl.ds(kept * dh, given * dh)], dst_ref=qbuf,
        send_sem=q_send.at[0], recv_sem=q_recv.at[0], device_id={"seq": far}, device_id_type=MESH,
    )

    scale = dh ** -0.5 * math.log2(math.e)
    rows = lax.broadcasted_iota(jnp.int32, (tok, tok), 0)
    cols = lax.broadcasted_iota(jnp.int32, (tok, tok), 1)
    causal = rows >= cols
    kmap2 = twice(pair(kmap_ref[0]), 0)

    def prepare(j):
        k, v = kbuf[j], vbuf[j]
        kt = k.T
        keys = stacked(kt * scale)
        k4t[j] = keys
        k2t[j] = jnp.concatenate(halves(kt), axis=0)
        v2 = pair(v)
        values = twice(v2, 0)
        v4[j] = values
        b, slope = softplus_and_slope(fold(dot(pair(k), kmap2)))
        sgk[j] = slope
        return keys, values, b, v2

    def diagonal(n, b, v):
        b4[n] = twice(pair(b), 0)
        b4t[n] = stacked(b.T)
        v4t[n] = stacked(v.T)

    def attend(group, keys, values, masked=False, fresh=False):
        scores = [dot(q4[h, :, : 3 * dh], keys[: 3 * dh]) for h in group]
        if not fresh:
            before = [(top[h], tot[h], acc[h]) for h in group]
        found = []
        for i, s in enumerate(scores):
            if masked:
                s = jnp.where(causal, s, NEGATIVE)
            new = jnp.max(s, axis=1, keepdims=True)
            if fresh:
                new = jnp.broadcast_to(new, (tok, dh))
            else:
                new = jnp.maximum(before[i][0], new)
                alpha = jnp.exp2(before[i][0] - new)
            p = jnp.exp2(s - twice(new, 1))
            hi, lo = halves(p)
            o = fold(dot(hi, values[:tok]) + dot(lo, values[:tok]))
            t = fold(p)
            if not fresh:
                t = before[i][1] * alpha + t
                o = before[i][2] * alpha + o
            found.append((new, t, o))
        for h, (new, t, o) in zip(group, found):
            top[h], tot[h], acc[h] = new, t, o

    def load_queries(slots, source):
        for h, q in zip(slots, source):
            q4[h] = twice(pair(q), 1)

    def before(slots, names, n, j, fresh):
        values = v4[j]
        acts = [fold(dot(q4[h, :, : 2 * dh], twice(pair(qmap_ref[m]), 0))) for h, m in zip(slots, names)]
        soft = [softplus_and_slope(act) for act in acts]
        a4s = [twice(pair(a), 1) for a, _ in soft]
        for h, (a, slope), four in zip(slots, soft, a4s):
            feat[h], sgq[h], a4[h] = a, slope, four
        kers = [jnp.where(causal, dot(four, b4t[n]), 0.0) for four in a4s]
        nums = [fold(dot(pair(ker), values)) for ker in kers]
        for h, ker, nm in zip(slots, kers, nums):
            den[h] = jnp.broadcast_to(jnp.sum(ker, axis=1, keepdims=True), (tok, dh))
            num[h] = nm
        attend(slots, k4t[j], values, masked=True, fresh=fresh)

    def own_queries(slots):
        return [q_ref[:, h * dh : (h + 1) * dh] for h in slots]

    state[...] = jnp.zeros_like(state)
    norm[...] = jnp.zeros_like(norm)
    adjns[...] = jnp.zeros_like(adjns)
    adjt2[...] = jnp.zeros_like(adjt2)
    _, _, b_own, v2_own = prepare(me)
    diagonal(0, b_own, v_ref[...])
    state_own = quad(dot_rows(pair(b_own), v2_own))
    norm_own = jnp.sum(b_own, axis=0, keepdims=True)

    def add_state(n, s, b):
        state[n] += s
        norm[n] += b

    def begin(slots):
        load_queries(slots, own_queries(slots))
        before(slots, slots, 0, me, True)

    cut = (kept + 1) // 2
    begin(main[:cut])
    pl.semaphore_wait(barrier, n_head + 4)
    msgs.start(*both("1+", "1-"))
    begin(main[cut:])
    msgs.start(*both("a+", "a-"))

    @pl.when(jnp.logical_not(early))
    def _():
        query_copy.start()

    @pl.when(early)
    def _():
        begin(rest)
        add_state(1, state_own, norm_own)

    msgs.arrived(*both("1+", "1-"))
    msgs.start(*both("1++", "1--", "b+", "b-"))
    msgs.arrived(*both("a+", "a-"))
    msgs.start(*both("a++", "a--", "c+", "c-"))

    @pl.when(early)
    def _():
        query_copy.wait_recv()
        load_queries(guest, [qbuf[:, i * dh : (i + 1) * dh] for i in range(given)])
        for h in guest:
            top[h] = jnp.full((tok, dh), NEGATIVE, F32)
            tot[h] = jnp.zeros((tok, dh), F32)
            acc[h] = jnp.zeros((tok, dh), F32)
        attend(guest, k4t[me], v4[me])

    def block(j):
        @pl.when(j < me)
        def _():
            keys, values, b, v2 = prepare(j)
            attend(main, keys, values)
            s, c = quad(dot_rows(pair(b), v2)), jnp.sum(b, axis=0, keepdims=True)
            add_state(0, s, c)
            add_state(1, s, c)

            @pl.when(early)
            def _():
                attend(rest + guest, keys, values)

        @pl.when(jnp.logical_and(j > me, j <= far))
        def _():
            keys, values, b, v2 = prepare(j)

            @pl.when(j < far)
            def _():
                attend(guest, keys, values)
                add_state(1, quad(dot_rows(pair(b), v2)), jnp.sum(b, axis=0, keepdims=True))

            @pl.when(j == far)
            def _():
                diagonal(1, b, vbuf[j])
                before(guest, rest, 1, j, False)

    order = (
        (0, 3), (0, 1), (3, 0), (1, 0), (0, 2), (2, 0), (3, 3), (3, 1), (1, 3), (1, 1),
        (3, 2), (1, 2), (2, 3), (2, 1), (2, 2),
    )

    def step(t, _):
        @pl.when(t == 4)
        def _():
            msgs.arrived(*both("1++", "1--"))
            msgs.start(*both("d+", "d-"))
            msgs.arrived(*both("a++", "a--"))

        @pl.when(t == 6)
        def _():
            msgs.arrived(*both("b+", "b-"))
            msgs.start(*both("b++", "b--"))

        @pl.when(t == 7)
        def _():
            msgs.arrived(*both("c+", "c-"))
            msgs.start(*both("c++", "c--"))

        @pl.when(t == 8)
        def _():
            msgs.arrived(*both("d+", "d-"))
            msgs.start(*both("d++", "d--"))

        @pl.when(t == 10)
        def _():
            msgs.arrived(*both("b++", "b--", "c++", "c--"))

        @pl.when(t == 14)
        def _():
            msgs.arrived(*both("d++", "d--"))

        dx, dz = jnp.int32(0), jnp.int32(0)
        for i, (ox, oz) in enumerate(order):
            dx = jnp.where(t == i, ox, dx)
            dz = jnp.where(t == i, oz, dz)
        block(at(dx, dz))
        return 0

    lax.fori_loop(0, n_seq - 1, step, 0)

    def after(slots, n):
        state2 = twice(pair(state[n]), 0)
        state2t = twice(pair(state[n].T), 0)
        norm_row = norm[n]
        feats = [feat[h] for h in slots]
        a2s = [a4[h, :, : 2 * dh] for h in slots]
        inter = [fold(dot(a2, state2)) for a2 in a2s]
        gns, gds = [], []
        for h, a, more in zip(slots, feats, inter):
            rden = 1.0 / (den[h] + jnp.sum(a * norm_row, axis=1, keepdims=True))
            student = (num[h] + more) * rden
            teacher = acc[h] / jnp.sum(tot[h], axis=1, keepdims=True)
            gn = (student - teacher) * rden
            gns.append(pair(gn))
            gds.append(-jnp.sum(gn * student, axis=1, keepdims=True))
        coups = [dot(twice(gn2, 1), v4t[n]) for gn2 in gns]
        c2s = [pair(jnp.where(causal, c + gd, 0.0)) for c, gd in zip(coups, gds)]
        gqs = [
            fold(dot(c2, b4[n])) + fold(dot(gn2, state2t)) + gd * norm_row
            for c2, gn2, gd in zip(c2s, gns, gds)
        ]
        grads = [quad(dot_rows(q4[h, :, : 2 * dh], pair(g * sgq[h]))) for h, g in zip(slots, gqs)]
        adj = sum(quad(dot_rows(a2, gn2)) for a2, gn2 in zip(a2s, gns))
        adjn = sum(jnp.sum(a * gd, axis=0, keepdims=True) for a, gd in zip(feats, gds))
        gkd = sum(quad(dot_rows(c2, a2)) for c2, a2 in zip(c2s, a2s))
        return grads, adj, adjn, gkd

    width = dh // n_seq
    groups = ((0, cut), (cut, heads - cut), (heads, 1))

    def rows_of(d):
        return pl.ds(pl.multiple_of(d * width, width), width)

    def scatter(g):
        first, count = groups[g]

        def send(k, _):
            peer = lax.rem(me + k, n_seq)
            pltpu.make_async_remote_copy(
                src_ref=grad.at[pl.ds(first, count), rows_of(peer)],
                dst_ref=parts.at[k - 1, pl.ds(first, count)],
                send_sem=rs_send.at[g], recv_sem=rs_recv.at[g],
                device_id={"seq": peer}, device_id_type=MESH,
            ).start()
            return 0

        lax.fori_loop(1, n_seq, send, 0)

    def all_of(ref, sem):
        pltpu.make_async_copy(ref, ref, sem).wait()

    def reduce(g):
        first, count = groups[g]
        span = pl.ds(first, count)
        all_of(parts.at[:, span], rs_recv.at[g])
        total = grad[span, rows_of(me)]
        for k in range(n_seq - 1):
            total = total + parts[k, span]
        mine[span] = total
        return jnp.sum(total * total, axis=0)

    def spread(g, first, count):
        span = pl.ds(first, count)
        whole[span, rows_of(me)] = mine[span]

        def send(k, _):
            pltpu.make_async_remote_copy(
                src_ref=mine.at[span],
                dst_ref=whole.at[span, rows_of(me)],
                send_sem=ag_send.at[g], recv_sem=ag_recv.at[g],
                device_id={"seq": lax.rem(me + k, n_seq)}, device_id_type=MESH,
            ).start()
            return 0

        lax.fori_loop(1, n_seq, send, 0)

    def keep(grads, slots):
        for h, g in zip(slots, grads):
            grad[h] = g

    grads, adj, adjn, gkd = after(main[:cut], 0)
    keep(grads, main[:cut])
    scatter(0)
    grads, adj_b, adjn_b, gkd_b = after(main[cut:], 0)
    keep(grads, main[cut:])
    adjs[...] = adj + adj_b
    adjns[0] = adjn + adjn_b
    gkds[0] = gkd + gkd_b

    @pl.when(early)
    def _():
        grads, adj, adjn, gkd = after(rest, 0)
        guests, adj_g, adjn_g, gkd_g = after(guest, 1)
        keep([u + w for u, w in zip(grads, guests)], rest)
        adjs[...] += adj + adj_g
        adjns[0] += adjn + adjn_g
        gkds[0] += gkd
        gkds[1] = gkd_g
        adjt2[1] = twice(pair(adj_g.T), 0)
        adjns[1] = adjn_g

    @pl.when(jnp.logical_not(early))
    def _():
        for h in rest:
            grad[h] = jnp.zeros((dh, dh), F32)

    scatter(1)

    adjt2[0] = twice(pair(adjs[...].T), 0)
    limit = jnp.where(early, far, me)

    def diagonal_grad(n, j):
        return quad(dot(k2t[j], pair(gkds[n] * sgk[j])))

    grad[heads] = diagonal_grad(0, me)

    @pl.when(early)
    def _():
        grad[heads] += diagonal_grad(1, far)

    batch = 8

    def later(c, _):
        js = [batch * c + i for i in range(batch)]
        inside = [j < limit for j in js]
        js = [jnp.where(ok, j, me) for ok, j in zip(inside, js)]
        which = [jnp.where(j < me, 0, 1) for j in js]
        outs = [fold(dot(v4[j, :tok], adjt2[w])) + adjns[w] for j, w in zip(js, which)]
        dks = [pair(jnp.where(ok, g * sgk[j], 0.0)) for ok, j, g in zip(inside, js, outs)]
        grad[heads] += quad(sum(dot(k2t[j], dk) for j, dk in zip(js, dks)))
        return 0

    lax.fori_loop(0, (limit + batch - 1) // batch, later, 0)
    scatter(2)
    early_squares = reduce(0) + reduce(1)
    spread(0, 0, heads)
    squares[0] = early_squares + reduce(2)

    def send_head(k, _):
        pltpu.make_async_remote_copy(
            src_ref=squares.at[0], dst_ref=head_squares.at[k - 1],
            send_sem=sq_send.at[0], recv_sem=sq_recv.at[0],
            device_id={"head": lax.rem(my_head + k, n_head)}, device_id_type=MESH,
        ).start()
        return 0

    def send_seq(k, _):
        pltpu.make_async_remote_copy(
            src_ref=squares.at[1], dst_ref=seq_squares.at[k - 1],
            send_sem=sq_send.at[1], recv_sem=sq_recv.at[1],
            device_id={"seq": lax.rem(me + k, n_seq)}, device_id_type=MESH,
        ).start()
        return 0

    lax.fori_loop(1, n_head, send_head, 0)
    spread(1, heads, 1)
    all_of(head_squares, sq_recv.at[0])
    squares[1] = squares[0] + jnp.sum(head_squares[...], axis=0)
    lax.fori_loop(1, n_seq, send_seq, 0)
    all_of(seq_squares, sq_recv.at[1])
    square = jnp.sum(squares[1] + jnp.sum(seq_squares[...], axis=0))
    size = (heads + 1) * n_head * dh * grad.shape[2]
    factor = 1.0 / jnp.sqrt(jnp.broadcast_to(square / size + EPSILON, (1, dh)))
    arrived = (parts.at[:, pl.ds(0, heads)], parts.at[:, pl.ds(heads, 1)])
    for g in range(2):
        all_of(arrived[g], ag_recv.at[g])
    gq_ref[...] = whole[pl.ds(0, heads)] * factor
    gk_ref[...] = whole[pl.ds(heads, 1)] * factor

    msgs.sent()

    @pl.when(jnp.logical_not(early))
    def _():
        query_copy.wait_send()

    for g in range(3):
        first, count = groups[g]
        all_of(parts.at[:, pl.ds(first, count)], rs_send.at[g])
    for g in range(2):
        all_of(arrived[g], ag_send.at[g])
    all_of(head_squares, sq_send.at[0])
    all_of(seq_squares, sq_send.at[1])


def on_device(queries, key_heads, value_heads, query_map, key_map):
    tok = queries.shape[0]
    heads, dh, feats = query_map.shape
    n = lax.axis_size("seq")
    given = heads // 8
    slots = heads + given
    return pl.pallas_call(
        kernel,
        out_shape=(jax.ShapeDtypeStruct((heads, dh, feats), F32), jax.ShapeDtypeStruct((1, dh, feats), F32)),
        in_specs=[pl.BlockSpec(memory_space=pltpu.VMEM)] * 5,
        out_specs=(pl.BlockSpec(memory_space=pltpu.VMEM),) * 2,
        scratch_shapes=[
            pltpu.VMEM((slots, tok, 4 * dh), BF16),
            pltpu.VMEM((n, 4 * dh, tok), BF16),
            pltpu.VMEM((n, 2 * tok, 2 * dh), BF16),
            pltpu.VMEM((n, 2 * dh, tok), BF16),
            pltpu.VMEM((n, tok, feats), F32),
            pltpu.VMEM((2, feats, dh), F32),
            pltpu.VMEM((2, 1, feats), F32),
        ] + [pltpu.VMEM((slots, tok, dh), F32)] * 6 + [
            pltpu.VMEM((slots, tok, 4 * feats), BF16),
            pltpu.VMEM((slots, tok, feats), F32),
            pltpu.VMEM((2, 2 * tok, 2 * feats), BF16),
            pltpu.VMEM((2, 4 * feats, tok), BF16),
            pltpu.VMEM((2, 4 * dh, tok), BF16),
            pltpu.VMEM((feats, dh), F32),
            pltpu.VMEM((2, 2 * dh, 2 * feats), BF16),
            pltpu.VMEM((2, 1, feats), F32),
            pltpu.VMEM((2, tok, feats), F32),
            pltpu.VMEM((n, tok, dh), F32),
            pltpu.VMEM((n, tok, dh), F32),
            pltpu.VMEM((tok, given * dh), F32),
            pltpu.VMEM((heads + 1, dh, feats), F32),
            pltpu.VMEM((n - 1, heads + 1, dh // n, feats), F32),
            pltpu.VMEM((heads + 1, dh // n, feats), F32),
            pltpu.VMEM((heads + 1, dh, feats), F32),
            pltpu.VMEM((2, dh // n, feats), F32),
            pltpu.VMEM((lax.axis_size("head") - 1, dh // n, feats), F32),
            pltpu.VMEM((n - 1, dh // n, feats), F32),
            pltpu.SemaphoreType.DMA((40,)),
            pltpu.SemaphoreType.DMA((40,)),
            pltpu.SemaphoreType.DMA((1,)),
            pltpu.SemaphoreType.DMA((1,)),
        ] + [pltpu.SemaphoreType.DMA((3,))] * 2 + [pltpu.SemaphoreType.DMA((2,))] * 4,
        compiler_params=pltpu.CompilerParams(vmem_limit_bytes=56 * 2**20, collective_id=0, has_side_effects=True),
    )(queries, key_heads, value_heads, query_map, key_map)


def solution(mesh):
    return jax.shard_map(
        on_device,
        mesh=mesh,
        in_specs=(P("seq", "head"), P("seq", "head"), P("seq", "head"), P("head"), P("head")),
        out_specs=(P("head"), P("head")),
        check_vma=False,
    )
```

```python
import math

import jax
import jax.numpy as jnp
from jax import lax
from jax.experimental import pallas as pl
from jax.experimental.pallas import tpu as pltpu
from jax.sharding import PartitionSpec as P

NEGATIVE = -1e30
EPSILON = 1e-06
F32 = jnp.float32
BF16 = jnp.bfloat16


def halves(x):
    hi = x.astype(BF16)
    return hi, (x - hi.astype(F32)).astype(BF16)


def pair(x):
    return jnp.concatenate(halves(x), axis=1)


def twice(x, axis):
    return jnp.concatenate([x, x], axis=axis)


def stacked(x):
    hi, lo = halves(x)
    return jnp.concatenate([hi, hi, lo, lo], axis=0)


def dot(a, b):
    return jnp.dot(a, b, preferred_element_type=F32)


def dot_rows(a, b):
    return lax.dot_general(a, b, (((0,), (0,)), ((), ())), preferred_element_type=F32)


def fold(x):
    w = x.shape[1] // 2
    return x[:, :w] + x[:, w:]


def quad(x):
    h = x.shape[0] // 2
    y = fold(x)
    return y[:h] + y[h:]


def softplus_and_slope(x):
    e = jnp.exp(-jnp.abs(x))
    soft = jnp.maximum(x, 0.0) + jnp.log1p(e)
    slope = jnp.where(x >= 0.0, 1.0, e) / (1.0 + e)
    return soft, slope


MESH = pl.DeviceIdType.MESH


class Messages:
    def __init__(self, send_sems, recv_sems):
        self.send_sems, self.recv_sems, self.all = send_sems, recv_sems, {}

    def make(self, name, ref, peer):
        at = len(self.all)
        self.all[name] = pltpu.make_async_remote_copy(
            src_ref=ref, dst_ref=ref, send_sem=self.send_sems.at[at], recv_sem=self.recv_sems.at[at],
            device_id={"seq": peer}, device_id_type=MESH,
        )

    def start(self, *names):
        for name in names:
            self.all[name].start()

    def arrived(self, *names):
        for name in names:
            self.all[name].wait_recv()

    def sent(self):
        for copy in self.all.values():
            copy.wait_send()


def kernel(q_ref, k_ref, v_ref, qmap_ref, kmap_ref, gq_ref, gk_ref,
           q4, k4t, v4, k2t, sgk, state, norm, acc, top, tot, num, den, feat, a4, sgq, b4, b4t, v4t, adjs, adjt2, adjns, gkds,
           kbuf, vbuf, qbuf, grad, parts, mine, whole, squares, head_squares, seq_squares,
           kv_send, kv_recv, q_send, q_recv, rs_send, rs_recv, ag_send, ag_recv, sq_send, sq_recv):
    heads, dh = qmap_ref.shape[0], qmap_ref.shape[1]
    tok = q_ref.shape[0]
    me = lax.axis_index("seq")
    my_head = lax.axis_index("head")
    n_seq, n_head = kbuf.shape[0], head_squares.shape[0] + 1
    side = math.isqrt(n_seq)
    my_x, my_z = me // side, lax.rem(me, side)
    given = qbuf.shape[1] // dh
    kept = heads - given
    far = n_seq - 1 - me
    early = me < n_seq // 2
    main = list(range(kept))
    rest = list(range(kept, heads))
    guest = list(range(heads, heads + given))

    def at(dx, dz):
        return lax.rem(my_x + dx + side, side) * side + lax.rem(my_z + dz + side, side)

    barrier = pltpu.get_barrier_semaphore()
    for peer in (at(1, 0), at(-1, 0), at(0, 1), at(0, -1), far):
        pl.semaphore_signal(barrier, inc=1, device_id={"seq": peer}, device_id_type=MESH)

    def greet_head(k, _):
        pl.semaphore_signal(barrier, inc=1, device_id={"head": lax.rem(my_head + k, n_head)}, device_id_type=MESH)
        return 0

    lax.fori_loop(1, n_head, greet_head, 0)
    kbuf[me] = k_ref[...]
    vbuf[me] = v_ref[...]

    half = tok // 2
    msgs = Messages(kv_send, kv_recv)
    for tag, buf, flip in (("k", kbuf, False), ("v", vbuf, True)):
        def place(a, b):
            return at(b, a) if flip else at(a, b)

        def route(name, a, b, first):
            up = place(1, 0) if first else place(0, 1)
            down = place(-1, 0) if first else place(0, -1)
            msgs.make(tag + name + "+", buf.at[place(a, b)], up)
            msgs.make(tag + name + "-", buf.at[place(a, b)], down)
            pa, pb, na, nb = (a - 1, b, a + 1, b) if first else (a, b - 1, a, b + 1)
            msgs.make(tag + name + "++", buf.at[place(pa, pb), pl.ds(0, half)], up)
            msgs.make(tag + name + "--", buf.at[place(na, nb), pl.ds(half, half)], down)

        route("1", 0, 0, True)
        for name, a in (("a", 0), ("b", -1), ("c", 1), ("d", 2)):
            route(name, a, 0, False)

    def both(*names):
        return [t + x for t in "kv" for x in names]

    query_copy = pltpu.make_async_remote_copy(
        src_ref=q_ref.at[:, pl.ds(kept * dh, given * dh)], dst_ref=qbuf,
        send_sem=q_send.at[0], recv_sem=q_recv.at[0], device_id={"seq": far}, device_id_type=MESH,
    )

    scale = dh ** -0.5 * math.log2(math.e)
    rows = lax.broadcasted_iota(jnp.int32, (tok, tok), 0)
    cols = lax.broadcasted_iota(jnp.int32, (tok, tok), 1)
    causal = rows >= cols
    kmap2 = twice(pair(kmap_ref[0]), 0)

    def prepare(j):
        k, v = kbuf[j], vbuf[j]
        kt = k.T
        keys = stacked(kt * scale)
        k4t[j] = keys
        k2t[j] = jnp.concatenate(halves(kt), axis=0)
        v2 = pair(v)
        values = twice(v2, 0)
        v4[j] = values
        b, slope = softplus_and_slope(fold(dot(pair(k), kmap2)))
        sgk[j] = slope
        return keys, values, b, v2

    def diagonal(n, b, v):
        b4[n] = twice(pair(b), 0)
        b4t[n] = stacked(b.T)
        v4t[n] = stacked(v.T)

    def attend(group, keys, values, masked=False, fresh=False):
        scores = [dot(q4[h, :, : 3 * dh], keys[: 3 * dh]) for h in group]
        if not fresh:
            before = [(top[h], tot[h], acc[h]) for h in group]
        found = []
        for i, s in enumerate(scores):
            if masked:
                s = jnp.where(causal, s, NEGATIVE)
            new = jnp.max(s, axis=1, keepdims=True)
            if fresh:
                new = jnp.broadcast_to(new, (tok, dh))
            else:
                new = jnp.maximum(before[i][0], new)
                alpha = jnp.exp2(before[i][0] - new)
            p = jnp.exp2(s - twice(new, 1))
            hi, lo = halves(p)
            o = fold(dot(hi, values[:tok]) + dot(lo, values[:tok]))
            t = fold(p)
            if not fresh:
                t = before[i][1] * alpha + t
                o = before[i][2] * alpha + o
            found.append((new, t, o))
        for h, (new, t, o) in zip(group, found):
            top[h], tot[h], acc[h] = new, t, o

    def load_queries(slots, source):
        for h, q in zip(slots, source):
            q4[h] = twice(pair(q), 1)

    def before(slots, names, n, j, fresh):
        values = v4[j]
        acts = [fold(dot(q4[h, :, : 2 * dh], twice(pair(qmap_ref[m]), 0))) for h, m in zip(slots, names)]
        soft = [softplus_and_slope(act) for act in acts]
        a4s = [twice(pair(a), 1) for a, _ in soft]
        for h, (a, slope), four in zip(slots, soft, a4s):
            feat[h], sgq[h], a4[h] = a, slope, four
        kers = [jnp.where(causal, dot(four, b4t[n]), 0.0) for four in a4s]
        nums = [fold(dot(pair(ker), values)) for ker in kers]
        for h, ker, nm in zip(slots, kers, nums):
            den[h] = jnp.broadcast_to(jnp.sum(ker, axis=1, keepdims=True), (tok, dh))
            num[h] = nm
        attend(slots, k4t[j], values, masked=True, fresh=fresh)

    def own_queries(slots):
        return [q_ref[:, h * dh : (h + 1) * dh] for h in slots]

    state[...] = jnp.zeros_like(state)
    norm[...] = jnp.zeros_like(norm)
    adjns[...] = jnp.zeros_like(adjns)
    adjt2[...] = jnp.zeros_like(adjt2)
    _, _, b_own, v2_own = prepare(me)
    diagonal(0, b_own, v_ref[...])
    state_own = quad(dot_rows(pair(b_own), v2_own))
    norm_own = jnp.sum(b_own, axis=0, keepdims=True)

    def add_state(n, s, b):
        state[n] += s
        norm[n] += b

    def begin(slots):
        load_queries(slots, own_queries(slots))
        before(slots, slots, 0, me, True)

    cut = (kept + 1) // 2
    begin(main[:cut])
    pl.semaphore_wait(barrier, n_head + 4)
    msgs.start(*both("1+", "1-"))
    begin(main[cut:])
    msgs.start(*both("a+", "a-"))

    @pl.when(jnp.logical_not(early))
    def _():
        query_copy.start()

    @pl.when(early)
    def _():
        begin(rest)
        add_state(1, state_own, norm_own)

    msgs.arrived(*both("1+", "1-"))
    msgs.start(*both("1++", "1--", "b+", "b-"))
    msgs.arrived(*both("a+", "a-"))
    msgs.start(*both("a++", "a--"))

    @pl.when(early)
    def _():
        query_copy.wait_recv()
        load_queries(guest, [qbuf[:, i * dh : (i + 1) * dh] for i in range(given)])
        for h in guest:
            top[h] = jnp.full((tok, dh), NEGATIVE, F32)
            tot[h] = jnp.zeros((tok, dh), F32)
            acc[h] = jnp.zeros((tok, dh), F32)
        attend(guest, k4t[me], v4[me])

    def block(j):
        @pl.when(j < me)
        def _():
            keys, values, b, v2 = prepare(j)
            attend(main, keys, values)
            s, c = quad(dot_rows(pair(b), v2)), jnp.sum(b, axis=0, keepdims=True)
            add_state(0, s, c)
            add_state(1, s, c)

            @pl.when(early)
            def _():
                attend(rest + guest, keys, values)

        @pl.when(jnp.logical_and(j > me, j <= far))
        def _():
            keys, values, b, v2 = prepare(j)

            @pl.when(j < far)
            def _():
                attend(guest, keys, values)
                add_state(1, quad(dot_rows(pair(b), v2)), jnp.sum(b, axis=0, keepdims=True))

            @pl.when(j == far)
            def _():
                diagonal(1, b, vbuf[j])
                before(guest, rest, 1, j, False)

    order = (
        (0, 3), (0, 1), (3, 0), (1, 0), (0, 2), (2, 0), (3, 3), (3, 1), (1, 3), (1, 1),
        (3, 2), (1, 2), (2, 3), (2, 1), (2, 2),
    )

    def step(t, _):
        @pl.when(t == 1)
        def _():
            msgs.start(*both("c+", "c-"))

        @pl.when(t == 4)
        def _():
            msgs.arrived(*both("1++", "1--"))
            msgs.start(*both("d+", "d-"))
            msgs.arrived(*both("a++", "a--"))

        @pl.when(t == 6)
        def _():
            msgs.arrived(*both("b+", "b-"))
            msgs.start(*both("b++", "b--"))

        @pl.when(t == 7)
        def _():
            msgs.arrived(*both("c+", "c-"))
            msgs.start(*both("c++", "c--"))

        @pl.when(t == 8)
        def _():
            msgs.arrived(*both("d+", "d-"))
            msgs.start(*both("d++", "d--"))

        @pl.when(t == 10)
        def _():
            msgs.arrived(*both("b++", "b--", "c++", "c--"))

        @pl.when(t == 14)
        def _():
            msgs.arrived(*both("d++", "d--"))

        dx, dz = jnp.int32(0), jnp.int32(0)
        for i, (ox, oz) in enumerate(order):
            dx = jnp.where(t == i, ox, dx)
            dz = jnp.where(t == i, oz, dz)
        block(at(dx, dz))
        return 0

    lax.fori_loop(0, n_seq - 1, step, 0)

    def after(slots, n):
        state2 = twice(pair(state[n]), 0)
        state2t = twice(pair(state[n].T), 0)
        norm_row = norm[n]
        feats = [feat[h] for h in slots]
        a2s = [a4[h, :, : 2 * dh] for h in slots]
        inter = [fold(dot(a2, state2)) for a2 in a2s]
        gns, gds = [], []
        for h, a, more in zip(slots, feats, inter):
            rden = 1.0 / (den[h] + jnp.sum(a * norm_row, axis=1, keepdims=True))
            student = (num[h] + more) * rden
            teacher = acc[h] / jnp.sum(tot[h], axis=1, keepdims=True)
            gn = (student - teacher) * rden
            gns.append(pair(gn))
            gds.append(-jnp.sum(gn * student, axis=1, keepdims=True))
        coups = [dot(twice(gn2, 1), v4t[n]) for gn2 in gns]
        c2s = [pair(jnp.where(causal, c + gd, 0.0)) for c, gd in zip(coups, gds)]
        gqs = [
            fold(dot(c2, b4[n])) + fold(dot(gn2, state2t)) + gd * norm_row
            for c2, gn2, gd in zip(c2s, gns, gds)
        ]
        grads = [quad(dot_rows(q4[h, :, : 2 * dh], pair(g * sgq[h]))) for h, g in zip(slots, gqs)]
        adj = sum(quad(dot_rows(a2, gn2)) for a2, gn2 in zip(a2s, gns))
        adjn = sum(jnp.sum(a * gd, axis=0, keepdims=True) for a, gd in zip(feats, gds))
        gkd = sum(quad(dot_rows(c2, a2)) for c2, a2 in zip(c2s, a2s))
        return grads, adj, adjn, gkd

    width = dh // n_seq
    groups = ((0, cut), (cut, heads - cut), (heads, 1))

    def rows_of(d):
        return pl.ds(pl.multiple_of(d * width, width), width)

    def scatter(g):
        first, count = groups[g]

        def send(k, _):
            peer = lax.rem(me + k, n_seq)
            pltpu.make_async_remote_copy(
                src_ref=grad.at[pl.ds(first, count), rows_of(peer)],
                dst_ref=parts.at[k - 1, pl.ds(first, count)],
                send_sem=rs_send.at[g], recv_sem=rs_recv.at[g],
                device_id={"seq": peer}, device_id_type=MESH,
            ).start()
            return 0

        lax.fori_loop(1, n_seq, send, 0)

    def all_of(ref, sem):
        pltpu.make_async_copy(ref, ref, sem).wait()

    def reduce(g):
        first, count = groups[g]
        span = pl.ds(first, count)
        all_of(parts.at[:, span], rs_recv.at[g])
        total = grad[span, rows_of(me)]
        for k in range(n_seq - 1):
            total = total + parts[k, span]
        mine[span] = total
        return jnp.sum(total * total, axis=0)

    def spread(g, first, count):
        span = pl.ds(first, count)
        whole[span, rows_of(me)] = mine[span]

        def send(k, _):
            pltpu.make_async_remote_copy(
                src_ref=mine.at[span],
                dst_ref=whole.at[span, rows_of(me)],
                send_sem=ag_send.at[g], recv_sem=ag_recv.at[g],
                device_id={"seq": lax.rem(me + k, n_seq)}, device_id_type=MESH,
            ).start()
            return 0

        lax.fori_loop(1, n_seq, send, 0)

    def keep(grads, slots):
        for h, g in zip(slots, grads):
            grad[h] = g

    grads, adj, adjn, gkd = after(main[:cut], 0)
    keep(grads, main[:cut])
    scatter(0)
    grads, adj_b, adjn_b, gkd_b = after(main[cut:], 0)
    keep(grads, main[cut:])
    adjs[...] = adj + adj_b
    adjns[0] = adjn + adjn_b
    gkds[0] = gkd + gkd_b

    @pl.when(early)
    def _():
        grads, adj, adjn, gkd = after(rest, 0)
        guests, adj_g, adjn_g, gkd_g = after(guest, 1)
        keep([u + w for u, w in zip(grads, guests)], rest)
        adjs[...] += adj + adj_g
        adjns[0] += adjn + adjn_g
        gkds[0] += gkd
        gkds[1] = gkd_g
        adjt2[1] = twice(pair(adj_g.T), 0)
        adjns[1] = adjn_g

    @pl.when(jnp.logical_not(early))
    def _():
        for h in rest:
            grad[h] = jnp.zeros((dh, dh), F32)

    scatter(1)

    adjt2[0] = twice(pair(adjs[...].T), 0)
    limit = jnp.where(early, far, me)

    def diagonal_grad(n, j):
        return quad(dot(k2t[j], pair(gkds[n] * sgk[j])))

    grad[heads] = diagonal_grad(0, me)

    @pl.when(early)
    def _():
        grad[heads] += diagonal_grad(1, far)

    batch = 8

    def later(c, _):
        js = [batch * c + i for i in range(batch)]
        inside = [j < limit for j in js]
        js = [jnp.where(ok, j, me) for ok, j in zip(inside, js)]
        which = [jnp.where(j < me, 0, 1) for j in js]
        outs = [fold(dot(v4[j, :tok], adjt2[w])) + adjns[w] for j, w in zip(js, which)]
        dks = [pair(jnp.where(ok, g * sgk[j], 0.0)) for ok, j, g in zip(inside, js, outs)]
        grad[heads] += quad(sum(dot(k2t[j], dk) for j, dk in zip(js, dks)))
        return 0

    lax.fori_loop(0, (limit + batch - 1) // batch, later, 0)
    scatter(2)
    early_squares = reduce(0) + reduce(1)
    spread(0, 0, heads)
    squares[0] = early_squares + reduce(2)

    def send_head(k, _):
        pltpu.make_async_remote_copy(
            src_ref=squares.at[0], dst_ref=head_squares.at[k - 1],
            send_sem=sq_send.at[0], recv_sem=sq_recv.at[0],
            device_id={"head": lax.rem(my_head + k, n_head)}, device_id_type=MESH,
        ).start()
        return 0

    def send_seq(k, _):
        pltpu.make_async_remote_copy(
            src_ref=squares.at[1], dst_ref=seq_squares.at[k - 1],
            send_sem=sq_send.at[1], recv_sem=sq_recv.at[1],
            device_id={"seq": lax.rem(me + k, n_seq)}, device_id_type=MESH,
        ).start()
        return 0

    lax.fori_loop(1, n_head, send_head, 0)
    spread(1, heads, 1)
    all_of(head_squares, sq_recv.at[0])
    squares[1] = squares[0] + jnp.sum(head_squares[...], axis=0)
    lax.fori_loop(1, n_seq, send_seq, 0)
    all_of(seq_squares, sq_recv.at[1])
    square = jnp.sum(squares[1] + jnp.sum(seq_squares[...], axis=0))
    size = (heads + 1) * n_head * dh * grad.shape[2]
    factor = 1.0 / jnp.sqrt(jnp.broadcast_to(square / size + EPSILON, (1, dh)))
    arrived = (parts.at[:, pl.ds(0, heads)], parts.at[:, pl.ds(heads, 1)])
    for g in range(2):
        all_of(arrived[g], ag_recv.at[g])
    gq_ref[...] = whole[pl.ds(0, heads)] * factor
    gk_ref[...] = whole[pl.ds(heads, 1)] * factor

    msgs.sent()

    @pl.when(jnp.logical_not(early))
    def _():
        query_copy.wait_send()

    for g in range(3):
        first, count = groups[g]
        all_of(parts.at[:, pl.ds(first, count)], rs_send.at[g])
    for g in range(2):
        all_of(arrived[g], ag_send.at[g])
    all_of(head_squares, sq_send.at[0])
    all_of(seq_squares, sq_send.at[1])


def on_device(queries, key_heads, value_heads, query_map, key_map):
    tok = queries.shape[0]
    heads, dh, feats = query_map.shape
    n = lax.axis_size("seq")
    given = heads // 8
    slots = heads + given
    return pl.pallas_call(
        kernel,
        out_shape=(jax.ShapeDtypeStruct((heads, dh, feats), F32), jax.ShapeDtypeStruct((1, dh, feats), F32)),
        in_specs=[pl.BlockSpec(memory_space=pltpu.VMEM)] * 5,
        out_specs=(pl.BlockSpec(memory_space=pltpu.VMEM),) * 2,
        scratch_shapes=[
            pltpu.VMEM((slots, tok, 4 * dh), BF16),
            pltpu.VMEM((n, 4 * dh, tok), BF16),
            pltpu.VMEM((n, 2 * tok, 2 * dh), BF16),
            pltpu.VMEM((n, 2 * dh, tok), BF16),
            pltpu.VMEM((n, tok, feats), F32),
            pltpu.VMEM((2, feats, dh), F32),
            pltpu.VMEM((2, 1, feats), F32),
        ] + [pltpu.VMEM((slots, tok, dh), F32)] * 6 + [
            pltpu.VMEM((slots, tok, 4 * feats), BF16),
            pltpu.VMEM((slots, tok, feats), F32),
            pltpu.VMEM((2, 2 * tok, 2 * feats), BF16),
            pltpu.VMEM((2, 4 * feats, tok), BF16),
            pltpu.VMEM((2, 4 * dh, tok), BF16),
            pltpu.VMEM((feats, dh), F32),
            pltpu.VMEM((2, 2 * dh, 2 * feats), BF16),
            pltpu.VMEM((2, 1, feats), F32),
            pltpu.VMEM((2, tok, feats), F32),
            pltpu.VMEM((n, tok, dh), F32),
            pltpu.VMEM((n, tok, dh), F32),
            pltpu.VMEM((tok, given * dh), F32),
            pltpu.VMEM((heads + 1, dh, feats), F32),
            pltpu.VMEM((n - 1, heads + 1, dh // n, feats), F32),
            pltpu.VMEM((heads + 1, dh // n, feats), F32),
            pltpu.VMEM((heads + 1, dh, feats), F32),
            pltpu.VMEM((2, dh // n, feats), F32),
            pltpu.VMEM((lax.axis_size("head") - 1, dh // n, feats), F32),
            pltpu.VMEM((n - 1, dh // n, feats), F32),
            pltpu.SemaphoreType.DMA((40,)),
            pltpu.SemaphoreType.DMA((40,)),
            pltpu.SemaphoreType.DMA((1,)),
            pltpu.SemaphoreType.DMA((1,)),
        ] + [pltpu.SemaphoreType.DMA((3,))] * 2 + [pltpu.SemaphoreType.DMA((2,))] * 4,
        compiler_params=pltpu.CompilerParams(vmem_limit_bytes=56 * 2**20, collective_id=0, has_side_effects=True),
    )(queries, key_heads, value_heads, query_map, key_map)


def solution(mesh):
    return jax.shard_map(
        on_device,
        mesh=mesh,
        in_specs=(P("seq", "head"), P("seq", "head"), P("seq", "head"), P("head"), P("head")),
        out_specs=(P("head"), P("head")),
        check_vma=False,
    )
```
